512 devices in a mesh: span: 16 (over y, x_lo), fsdp: 32 (over x_hi, z, core).
Axes of the slice: x: 4 (x_hi: 2, x_lo: 2; x = x_hi * 2 + x_lo), y: 8, z: 8, core: 2. Of those that a mesh axis runs over, the one named last changes fastest.
Arguments:
- tokens: bfloat16 [8192, 6144], P('span', 'fsdp'), may hold values from -64 to 64
- queries: bfloat16 [8192, 4096], P('span', 'fsdp'), may hold values from -12 to 12
- key_weight: bfloat16 [6144, 4096], P('span', 'fsdp'), may hold values from -0.076546554 to 0.076546554
- value_weight: bfloat16 [6144, 4096], P('span', 'fsdp'), may hold values from -0.078125 to 0.078125
- modulation: bfloat16 [8, 12288], replicated, may hold values from -3 to 3
- levels: int32 [16], replicated, may hold values from 0 to 7
- visible: int32 [16, 16], replicated, may hold values from 0 to 1, as said below
- counts: int32 [16], replicated, may hold values from 256 to 512, as said below
Outputs:
- attended: bfloat16 [8192, 4096], P('span', 'fsdp')
The draws below stay inside these ranges and needn't reach their ends.
Inputs may be any that keep to these rules, and one draw needn't show every extreme that they name: visible[c, b] is 1 only where b < c, and always where b = c - 1. The live tokens of a span are its first counts[c] slots; some span is full.
All inputs are finite; a program needn't handle non-finite values.
Results may differ from the reference program's by a relative error of at most 0.0078.
Values may be sent and summed in bfloat16 or wider, within the bound.
No kernel may reach another device: no remote copies, remote signals or barrier semaphores. Data moves between devices by JAX's collectives and lax.ppermute only.
A program may use at most 64 MiB of HBM per device.

```python
import math
import jax
import jax.numpy as jnp
from jax import lax

D = 6144
HD = 128
LEVELS = 8
SPAN_TOK = 512
HEADS = 32
SPANS = 16
TOKENS = 8192


def draw_tokens(key, part):
    key = jax.random.fold_in(key, 5)
    base_key, rough_key = jax.random.split(key, 2)
    position = jnp.arange(D, dtype=jnp.float32) / D
    rough = jax.random.uniform(rough_key, (D,), jnp.float32, 0.5, 1.5)
    spread = jnp.exp(position * math.log(4.0)) * rough
    centre = 1.5 * position
    base = jnp.clip(jax.random.normal(base_key, (TOKENS, D), jnp.float32), -6.0, 6.0)
    return (base * spread[None, :] + centre[None, :]).astype(jnp.bfloat16)


def draw_queries(key, part):
    key = jax.random.fold_in(key, 31)
    result = jnp.clip(2.5 * jax.random.normal(key, (TOKENS, HEADS * HD), jnp.float32), -12.0, 12.0)
    return result.astype(jnp.bfloat16)


def draw_key_weight(key, part):
    key = jax.random.fold_in(key, 37)
    base = jnp.clip(jax.random.normal(key, (D, HEADS * HD), jnp.float32), -5.0, 5.0) * D ** (-0.5)
    result = base
    return result.astype(jnp.bfloat16)


def draw_visible(key, part):
    key = jax.random.fold_in(key, 11)
    random_bits = jax.random.randint(key, (SPANS, SPANS), 0, 2, dtype=jnp.int32)
    row_ids = jnp.arange(SPANS, dtype=jnp.int32)[:, None]
    col_ids = jnp.arange(SPANS, dtype=jnp.int32)[None, :]
    earlier = jnp.where(col_ids < row_ids - 1, random_bits, 0)
    return jnp.where(col_ids == row_ids - 1, 1, earlier).astype(jnp.int32)


def draw_counts(key, part):
    key = jax.random.fold_in(key, 23)
    first_key, second_key = jax.random.split(key)
    missing = jax.random.randint(first_key, (SPANS,), 0, SPAN_TOK // 2 + 1, dtype=jnp.int32)
    full_span = jax.random.randint(second_key, (), 0, SPANS, dtype=jnp.int32)
    missing = jnp.where(jnp.arange(SPANS, dtype=jnp.int32) == full_span, 0, missing)
    return (SPAN_TOK - missing).astype(jnp.int32)


def place_ends(entries, rng, smallest, top_value):
    longest = entries.shape.index(max(entries.shape))
    spots = []
    for shift in (0, 1):
        where = [jax.random.randint(jax.random.fold_in(rng, axis), (), 0, length) for axis, length in enumerate(entries.shape)]
        where[longest] = (where[longest] + shift) % entries.shape[longest]
        spots.append(tuple(where))
    return entries.at[spots[0]].set(smallest).at[spots[1]].set(top_value)


def shard_levels(own_key, shape, cuts, least, largest):
    factor_of = 1.0
    for axis_at, parts in cuts:
        draws = jax.random.uniform(jax.random.fold_in(jax.random.fold_in(own_key, 6), axis_at), (parts,), jnp.float32, least / len(cuts), largest / len(cuts))
        factor_of = factor_of * jnp.repeat(jnp.exp(draws), shape[axis_at] // parts).reshape((-1,) + (1,) * (len(shape) - 1 - axis_at))
    return factor_of


def gaussian(rng, dims, scale, bound, cuts=(), held_as=jnp.bfloat16):
    level = shard_levels(rng, dims, cuts, -0.22, 0.18) if cuts else 1.0
    drawn = jax.random.normal(rng, dims, jnp.float32) * scale * level
    return jnp.minimum(jnp.maximum(drawn, -bound), bound).astype(held_as)


def setup_inputs(seed: int = 0) -> dict:
    arg_keys = jax.random.split(jax.random.key(seed), 9)
    return {
        "tokens": draw_tokens(jax.random.fold_in(arg_keys[8], 71), 0),
        "queries": draw_queries(jax.random.fold_in(arg_keys[8], 71), 0),
        "key_weight": draw_key_weight(jax.random.fold_in(arg_keys[8], 71), 0),
        "value_weight": gaussian(arg_keys[3], (D, HEADS * HD), D ** -0.5, 0.078125, ((0, 16), (1, 32))),
        "modulation": gaussian(arg_keys[4], (LEVELS, 2 * D), 0.5, 3.0),
        "levels": place_ends(jax.random.randint(arg_keys[5], (SPANS,), 0, LEVELS), jax.random.fold_in(arg_keys[5], 1), 0, LEVELS - 1).astype(jnp.int32),
        "visible": draw_visible(jax.random.fold_in(arg_keys[8], 71), 0),
        "counts": draw_counts(jax.random.fold_in(arg_keys[8], 71), 0),
    }


neg_big = -1e+30
epsilon = 1e-06

def reference(tokens, queries, key_weight, value_weight, modulation, levels, visible, counts):
    level_hot = (levels[:, None] == jnp.arange(LEVELS, dtype=jnp.int32)[None, :]).astype(jnp.bfloat16)
    mod_rows = jnp.dot(level_hot, modulation, preferred_element_type=jnp.float32)
    shift_rows = jnp.repeat(mod_rows[:, :D], SPAN_TOK, axis=0)
    scale_rows = jnp.repeat(mod_rows[:, D:], SPAN_TOK, axis=0)
    widened = tokens.astype(jnp.float32)
    row_mean = lax.optimization_barrier(jnp.sum(widened, axis=1, keepdims=True)) / D
    variance = lax.optimization_barrier(jnp.sum(widened * widened, axis=1, keepdims=True)) / D - row_mean * row_mean
    normed = ((widened - row_mean) * lax.rsqrt(variance + epsilon) * (1.0 + scale_rows) + shift_rows).astype(jnp.bfloat16)
    key_rows = jnp.dot(normed, key_weight, preferred_element_type=jnp.float32).astype(jnp.bfloat16)
    value_rows = jnp.dot(normed, value_weight, preferred_element_type=jnp.float32).astype(jnp.bfloat16)
    key_heads = key_rows.reshape(TOKENS, HEADS, HD).transpose(1, 0, 2)
    value_heads = value_rows.reshape(TOKENS, HEADS, HD).transpose(1, 0, 2)
    query_heads = queries.reshape(SPANS, SPAN_TOK, HEADS, HD).transpose(0, 2, 1, 3)
    key_pos = jnp.arange(TOKENS, dtype=jnp.int32)
    key_span = key_pos // SPAN_TOK
    key_live = key_pos - key_span * SPAN_TOK < counts[key_span]

    def one_span(span_item):
        span_index, query_span = span_item
        seen_spans = jnp.where(jnp.arange(SPANS, dtype=jnp.int32) == span_index, 1, visible[span_index])
        valid_keys = key_live & (seen_spans[key_span] == 1)

        def one_head(head_item):
            query_head, key_head, value_head = head_item
            scores = jnp.dot(query_head, key_head.T, preferred_element_type=jnp.float32)
            scores = jnp.where(valid_keys[None, :], scores * HD ** (-0.5), neg_big)
            row_max = lax.optimization_barrier(jnp.max(scores, axis=1, keepdims=True))
            weights = jnp.where(valid_keys[None, :], jnp.exp(scores - row_max), 0.0)
            row_total = lax.optimization_barrier(jnp.sum(weights, axis=1, keepdims=True))
            return jnp.dot(weights.astype(jnp.bfloat16), value_head, preferred_element_type=jnp.float32) / row_total
        attended = lax.map(one_head, (query_span, key_heads, value_heads))
        live_rows = jnp.arange(SPAN_TOK, dtype=jnp.int32) < counts[span_index]
        attended = jnp.where(live_rows[None, :, None], attended, 0.0)
        return attended.transpose(1, 0, 2).reshape(SPAN_TOK, HEADS * HD).astype(jnp.bfloat16)
    result = lax.map(one_span, (jnp.arange(SPANS, dtype=jnp.int32), query_heads))
    return result.reshape(TOKENS, HEADS * HD)
```

```python
import functools

import jax
import jax.numpy as jnp
from jax import lax
from jax.experimental import pallas as pl
from jax.experimental.pallas import tpu as pltpu
from jax.sharding import Mesh, PartitionSpec as P

HD = 128
EPSILON = 1e-06
NEG_BIG = -1e30
LOG2E = 1.4426950408889634
SPAN_AXES = ("yh", "yl", "xl")
FSDP_AXES = ("xh", "z", "c")
SIZES = (4, 2, 2, 2, 8, 2)
QUAD = 4
STAT_ROWS = 16

VMEM = pl.BlockSpec(memory_space=pltpu.VMEM)
SMEM = pl.BlockSpec(memory_space=pltpu.SMEM)


def params(mib=24):
    return pltpu.CompilerParams(vmem_limit_bytes=mib * 1024 * 1024)


def shifted(value, axis, size, by):
    return lax.ppermute(value, axis, [(i, (i + by) % size) for i in range(size)])


def sums_kernel(count, *refs):
    out = refs[-1]
    total = jnp.zeros((1, out.shape[1]), jnp.float32)
    square = jnp.zeros((1, out.shape[1]), jnp.float32)
    for ref in refs[:count]:
        block = ref[...].astype(jnp.float32)
        total += jnp.sum(block, axis=0, keepdims=True)
        square += jnp.sum(block * block, axis=0, keepdims=True)
    if len(refs) > count + 1:
        total += refs[count][0:1, :]
        square += refs[count][1:2, :]
    out[...] = jnp.zeros_like(out)
    out[0:1, :] = total
    out[1:2, :] = square


def row_sums(pieces, earlier=None):
    rest = () if earlier is None else (earlier,)
    width = pieces[0].shape[1]
    return pl.pallas_call(
        functools.partial(sums_kernel, len(pieces)),
        out_shape=jax.ShapeDtypeStruct((8, width), jnp.float32),
        in_specs=[VMEM] * (len(pieces) + len(rest)),
        out_specs=VMEM,
        compiler_params=params(),
    )(*pieces, *rest)


def gathered_weights(index_ref, w_ref, head, group):
    blocks = []
    for offset in (2 * group, 2 * group + 1):
        blocks.append(w_ref[index_ref[offset], head])
        blocks.append(w_ref[index_ref[8 + offset], head])
    return jnp.concatenate(blocks, axis=0)


def norm_kernel(
    index_ref, own_ref, other_ref, scale_ref, shift_ref,
    a0, b0, r1u, r2u, r3u, r4u, r5u, r1d, r2d, r3d, r4d, r5d,
    w_ref, normed_ref, part_ref,
):
    model_width = 2.0 * normed_ref.shape[1]
    stats = own_ref[...] + other_ref[...]
    mean = stats[0:1, :] / model_width
    variance = stats[1:2, :] / model_width - mean * mean
    rstd = lax.rsqrt(variance + EPSILON)
    columns = jnp.transpose(jnp.concatenate([mean, rstd, jnp.zeros((6, mean.shape[1]), jnp.float32)], axis=0))
    mean_col, rstd_col = columns[:, 0:1], columns[:, 1:2]
    feats = a0.shape[0]
    half = feats // 2
    two = 2 * feats
    pairs = [
        [a0[...], b0[...]],
        [r1u[...], r2u[feats:two, :]],
        [r2u[0:feats, :], r3u[feats:two, :]],
        [r3u[0:feats, :], r4u[half : half + feats, :]],
        [r4d[feats : feats + half, :], r4u[0:half, :], r5d[...], r5u[...]],
        [r3d[feats:two, :], r4d[0:feats, :]],
        [r2d[feats:two, :], r3d[0:feats, :]],
        [r1d[...], r2d[0:feats, :]],
    ]
    for offset, pair in enumerate(pairs):
        block = jnp.transpose(jnp.concatenate(pair, axis=0)).astype(jnp.float32)
        block = (block - mean_col) * rstd_col * (1.0 + scale_ref[offset : offset + 1, :]) + shift_ref[
            offset : offset + 1, :
        ]
        normed_ref[:, offset * two : (offset + 1) * two] = block.astype(jnp.bfloat16)
    project(index_ref, 17, normed_ref, w_ref, part_ref)


def project(index_ref, which, normed_ref, w_ref, part_ref):
    head = index_ref[which]
    for group in range(4):
        depth = normed_ref.shape[1] // 4
        product = jnp.dot(
            normed_ref[:, group * depth : (group + 1) * depth],
            gathered_weights(index_ref, w_ref, head, group),
            preferred_element_type=jnp.float32,
        )
        if group == 0:
            part_ref[...] = product
        else:
            part_ref[...] += product


def keep_kernel(index_ref, normed_ref, w_ref, part_ref):
    project(index_ref, 16, normed_ref, w_ref, part_ref)


def join_kernel(mine_ref, theirs_ref, out_ref):
    rows = mine_ref.shape[0]
    total = (mine_ref[...] + theirs_ref[...]).astype(jnp.bfloat16)
    keys = total[:, 0:HD]
    blocks = [jnp.transpose(total[b * HD : (b + 1) * HD, HD : 2 * HD]) for b in range(rows // HD)]
    packed = jnp.concatenate([keys] + blocks, axis=0)
    for copy in range(out_ref.shape[0]):
        out_ref[copy] = packed


def attend_kernel(seen_ref, live_ref, q_ref, kv_ref, out_ref, q_t, best, total, acc):
    span_len = q_ref.shape[1]
    factor = LOG2E * HD ** (-0.5)
    for i in range(QUAD):
        q_t[...] = jnp.transpose(q_ref[i])
        best[...] = jnp.full_like(best, NEG_BIG)
        total[...] = jnp.zeros_like(total)
        acc[...] = jnp.zeros_like(acc)
        for j in range(QUAD):

            @pl.when(seen_ref[i, j] == 1)
            def _():
                scores = jnp.dot(kv_ref[j, 0:span_len, :], q_t[...], preferred_element_type=jnp.float32)
                live = lax.broadcasted_iota(jnp.int32, scores.shape, 0) < live_ref[j]
                scores = jnp.where(live, scores * factor, NEG_BIG)
                top = jnp.maximum(best[0:1, :], jnp.max(scores, axis=0, keepdims=True))
                weights = jnp.where(live, jnp.exp2(scores - top), 0.0)
                fading = jnp.exp2(best[0:1, :] - top)
                total[0:1, :] = total[0:1, :] * fading + jnp.sum(weights, axis=0, keepdims=True)
                best[0:1, :] = top
                values = jnp.concatenate(
                    [kv_ref[j, span_len + b * HD : span_len + (b + 1) * HD, :] for b in range(span_len // HD)],
                    axis=1,
                )
                acc[...] = acc[...] * fading + jnp.dot(
                    values, weights.astype(jnp.bfloat16), preferred_element_type=jnp.float32
                )

        out_ref[i, 0:HD, :] = acc[...].astype(jnp.bfloat16)
        rows = []
        for value in (best[0:1, :], total[0:1, :]):
            for _part in range(3):
                part = value.astype(jnp.bfloat16).astype(jnp.float32)
                rows.append(part)
                value = value - part
        rows.append(jnp.zeros((STAT_ROWS - 6, span_len), jnp.float32))
        out_ref[i, HD : HD + STAT_ROWS, :] = jnp.concatenate(rows, axis=0).astype(jnp.bfloat16)


def merge_kernel(live_ref, part_ref, out_ref):
    span_len = out_ref.shape[0]
    bests, totals = [], []
    for j in range(QUAD):
        stat = part_ref[j, HD : HD + STAT_ROWS, :].astype(jnp.float32)
        bests.append((stat[0:1] + stat[1:2]) + stat[2:3])
        totals.append((stat[3:4] + stat[4:5]) + stat[5:6])
    top = functools.reduce(jnp.maximum, bests)
    share = [jnp.exp2(b - top) for b in bests]
    total = sum(s * t for s, t in zip(share, totals))
    result = sum(s * part_ref[j, 0:HD, :].astype(jnp.float32) for j, s in enumerate(share))
    slot = lax.broadcasted_iota(jnp.int32, total.shape, 1)
    result = jnp.where(slot < live_ref[0], result / total, 0.0)
    out_ref[...] = jnp.transpose(result).astype(jnp.bfloat16)


def on_device(tokens, queries, key_weight, value_weight, modulation, levels, visible, counts):
    span_id = lax.axis_index(SPAN_AXES)
    quad = lax.axis_index("yh")
    place = lax.axis_index(("yl", "xl"))
    xh, z, core = lax.axis_index("xh"), lax.axis_index("z"), lax.axis_index("c")
    span_len, feats = tokens.shape
    depth = key_weight.shape[0]
    half = feats // 2

    both = jnp.concatenate([key_weight, value_weight], axis=1).reshape(2, depth // 2, 2 * HD)
    spread = jnp.broadcast_to(both[None], (2, 2, depth // 2, 2 * HD)).reshape(4, depth // 2, 2 * HD)
    local_w = lax.all_to_all(spread, ("xl", "c"), 0, 0, tiled=True)
    all_w = lax.all_gather(local_w, ("yh", "yl"), axis=0, tiled=True).reshape(16, 2, depth // 2, 2 * HD)

    a0 = jnp.transpose(tokens)
    up = functools.partial(shifted, axis="z", size=8, by=1)
    down = functools.partial(shifted, axis="z", size=8, by=-1)
    r1u, r1d = up(a0), down(a0)
    b0 = shifted(a0, "xh", 2, 1)
    r2u, r2d = up(jnp.concatenate([r1u, b0], axis=0)), down(jnp.concatenate([b0, r1d], axis=0))
    r3u, r3d = up(r2u), down(r2d)
    r4u, r4d = up(r3u[half:]), down(r3d[: half + feats])
    r5u, r5d = up(r4u[feats:]), down(r4d[:half])
    early = row_sums([a0, b0, r1u, r1d, r2u, r2d, r3u, r3d])
    own_sums = row_sums([r4u, r4d, r5u, r5d], early)
    other_sums = shifted(own_sums, "c", 2, 1)

    mod_row = lax.dynamic_index_in_dim(modulation, levels[span_id], 0, keepdims=False)
    table = mod_row.reshape(2, 2, 8, 2, feats)
    table = lax.dynamic_index_in_dim(table, core, 3, keepdims=False)
    ring_z = (z - jnp.arange(8, dtype=jnp.int32)) % 8
    ring_x = jnp.stack([xh, 1 - xh])
    table = jnp.take(jnp.take(table, ring_x, axis=1), ring_z, axis=2)
    table = jnp.transpose(table, (0, 2, 1, 3)).reshape(2, 8, 2 * feats).astype(jnp.float32)
    index = jnp.concatenate(
        [xh * 8 + ring_z, (1 - xh) * 8 + ring_z, jnp.stack([core, 1 - core])]
    ).astype(jnp.int32)

    part_type = jax.ShapeDtypeStruct((span_len, 2 * HD), jnp.float32)
    normed, theirs = pl.pallas_call(
        norm_kernel,
        out_shape=(jax.ShapeDtypeStruct((span_len, 16 * feats), jnp.bfloat16), part_type),
        in_specs=[SMEM] + [VMEM] * 17,
        out_specs=(VMEM, VMEM),
        compiler_params=params(32),
    )(index, own_sums, other_sums, table[1], table[0], a0, b0, r1u, r2u, r3u, r4u, r5u, r1d, r2d, r3d, r4d, r5d, all_w)
    received = shifted(theirs, "c", 2, 1)
    mine = pl.pallas_call(
        keep_kernel,
        out_shape=part_type,
        in_specs=[SMEM, VMEM, VMEM],
        out_specs=VMEM,
        compiler_params=params(),
    )(index, normed, all_w)
    packed = pl.pallas_call(
        join_kernel,
        out_shape=jax.ShapeDtypeStruct((QUAD, 2 * span_len, HD), jnp.bfloat16),
        in_specs=[VMEM, VMEM],
        out_specs=VMEM,
        compiler_params=params(),
    )(mine, received)

    kv = lax.all_to_all(packed, ("yl", "xl"), 0, 0, tiled=True)
    q_all = lax.all_to_all(jnp.broadcast_to(queries[None], (QUAD, span_len, HD)), "yh", 0, 0, tiled=True)
    q_spans = jnp.arange(QUAD, dtype=jnp.int32) * QUAD + place
    k_spans = jnp.arange(QUAD, dtype=jnp.int32) + QUAD * quad
    seen = jnp.where(q_spans[:, None] == k_spans[None, :], 1, visible[q_spans][:, k_spans]).astype(jnp.int32)
    partial = pl.pallas_call(
        attend_kernel,
        out_shape=jax.ShapeDtypeStruct((QUAD, HD + STAT_ROWS, span_len), jnp.bfloat16),
        in_specs=[SMEM, SMEM, VMEM, VMEM],
        out_specs=VMEM,
        scratch_shapes=[
            pltpu.VMEM((HD, span_len), jnp.bfloat16),
            pltpu.VMEM((8, span_len), jnp.float32),
            pltpu.VMEM((8, span_len), jnp.float32),
            pltpu.VMEM((HD, span_len), jnp.float32),
        ],
        compiler_params=params(),
    )(seen, counts[k_spans], q_all, kv)
    parts = lax.all_to_all(partial, "yh", 0, 0, tiled=True)
    return pl.pallas_call(
        merge_kernel,
        out_shape=jax.ShapeDtypeStruct((span_len, HD), jnp.bfloat16),
        in_specs=[SMEM, VMEM],
        out_specs=VMEM,
        compiler_params=params(),
    )(lax.dynamic_slice_in_dim(counts, span_id, 1), parts)


def solution(mesh):
    fine = Mesh(mesh.devices.reshape(SIZES), SPAN_AXES + FSDP_AXES)
    spread = P(SPAN_AXES, FSDP_AXES)
    return jax.shard_map(
        on_device,
        mesh=fine,
        in_specs=(spread, spread, spread, spread, P(), P(), P(), P()),
        out_specs=spread,
        check_vma=False,
    )
```

```python
import functools

import jax
import jax.numpy as jnp
from jax import lax
from jax.experimental import pallas as pl
from jax.experimental.pallas import tpu as pltpu
from jax.sharding import Mesh, PartitionSpec as P

HD = 128
EPSILON = 1e-06
NEG_BIG = -1e30
LOG2E = 1.4426950408889634
SPAN_AXES = ("yh", "yl", "xl")
FSDP_AXES = ("xh", "z", "c")
SIZES = (4, 2, 2, 2, 8, 2)
QUAD = 4
RING = 8
STAT_ROWS = 16
SPAN, YH, PLACE, Y, XL, XH, Z, CORE, LEVEL = range(9)

VMEM = pl.BlockSpec(memory_space=pltpu.VMEM)
SMEM = pl.BlockSpec(memory_space=pltpu.SMEM)
ANY = pl.BlockSpec(memory_space=pl.ANY)


def params(mib=24):
    return pltpu.CompilerParams(vmem_limit_bytes=mib * 1024 * 1024)


def shifted(value, axis, size, by):
    return lax.ppermute(value, axis, [(i, (i + by) % size) for i in range(size)])


def moved(value, by):
    return lax.ppermute(value, "yh", [(i, i + by) for i in range(QUAD) if 0 <= i + by < QUAD])


def fetch(refs, held, sems):
    copies = [pltpu.make_async_copy(ref, held.at[k], sems.at[k]) for k, ref in enumerate(refs)]
    for copy in copies:
        copy.start()
    return copies


def split_kernel(ids_ref, key_ref, value_ref, own_ref, other_ref):
    rows = own_ref.shape[0]
    for part, out in ((ids_ref[CORE], own_ref), (1 - ids_ref[CORE], other_ref)):
        first = pl.multiple_of(part * rows, 16)
        out[:, 0:HD] = key_ref[pl.ds(first, rows), :]
        out[:, HD : 2 * HD] = value_ref[pl.ds(first, rows), :]


def sums_kernel(count, has_earlier, *refs):
    pieces = refs[:count]
    out, held, sems = refs[-3], refs[-2], refs[-1]
    copies = fetch(pieces, held, sems)
    total = jnp.zeros((1, out.shape[1]), jnp.float32)
    square = jnp.zeros((1, out.shape[1]), jnp.float32)
    for k, copy in enumerate(copies):
        copy.wait()
        block = held[k].astype(jnp.float32)
        total += jnp.sum(block, axis=0, keepdims=True)
        square += jnp.sum(block * block, axis=0, keepdims=True)
    if has_earlier:
        total += refs[count][0:1, :]
        square += refs[count][1:2, :]
    out[...] = jnp.zeros_like(out)
    out[0:1, :] = total
    out[1:2, :] = square


def row_sums(pieces, earlier=None):
    rest = () if earlier is None else (earlier,)
    rows, width = pieces[0].shape
    return pl.pallas_call(
        functools.partial(sums_kernel, len(pieces), bool(rest)),
        out_shape=jax.ShapeDtypeStruct((8, width), jnp.float32),
        in_specs=[ANY] * len(pieces) + [VMEM] * len(rest),
        out_specs=VMEM,
        scratch_shapes=[
            pltpu.VMEM((len(pieces), rows, width), pieces[0].dtype),
            pltpu.SemaphoreType.DMA((len(pieces),)),
        ],
        compiler_params=params(),
    )(*pieces, *rest)


def norm_kernel(ids_ref, own_ref, other_ref, table_ref, *refs):
    pieces = refs[:RING]
    normed_ref, held, sems = refs[RING:]
    copies = fetch(pieces, held, sems)
    feats = held.shape[1] // 2
    model_width = 4.0 * RING * feats
    stats = own_ref[...] + other_ref[...]
    mean = stats[0:1, :] / model_width
    variance = stats[1:2, :] / model_width - mean * mean
    rstd = lax.rsqrt(variance + EPSILON)
    columns = jnp.transpose(jnp.concatenate([mean, rstd, jnp.zeros((6, mean.shape[1]), jnp.float32)], axis=0))
    mean_col, rstd_col = columns[:, 0:1], columns[:, 1:2]
    blocks = table_ref.shape[0] // 2
    for slot, copy in enumerate(copies):
        copy.wait()
        for part in range(2):
            x_at = jnp.where(part == 0, ids_ref[XH], 1 - ids_ref[XH])
            z_at = lax.rem(ids_ref[Z] + slot, RING)
            row = x_at * (2 * RING) + z_at * 2 + ids_ref[CORE]
            shift = table_ref[pl.ds(row, 1), :]
            scale = table_ref[pl.ds(blocks + row, 1), :]
            block = jnp.transpose(held[slot, part * feats : (part + 1) * feats, :]).astype(jnp.float32)
            block = (block - mean_col) * rstd_col * (1.0 + scale) + shift
            normed_ref[slot, part] = block.astype(jnp.bfloat16)


def add_products(ids_ref, normed_ref, weights, slot, parts):
    y_at = lax.rem(ids_ref[Y] + slot, RING)
    half = y_at // (RING // 2)
    part = jnp.where(half == ids_ref[XH], 0, 1)
    for head in range(2):
        for side in range(2):
            xl_at = ids_ref[XL] if side == 0 else 1 - ids_ref[XL]
            z_at = 2 * (y_at - half * (RING // 2)) + xl_at
            place = lax.rem(z_at + RING - ids_ref[Z], RING)
            product = jnp.dot(normed_ref[place, part], weights[2 * side + head], preferred_element_type=jnp.float32)
            parts[head] = product if parts[head] is None else parts[head] + product


def project_kernel(slots, has_earlier, ids_ref, normed_ref, *refs):
    pieces = refs[: len(slots)]
    out_keep, out_send, held, sems = refs[-4:]
    copies = fetch(pieces, held, sems)
    if has_earlier:
        parts = [refs[len(slots)][...], refs[len(slots) + 1][...]]
    else:
        parts = [None, None]
    for k, slot in enumerate(slots):
        copies[k].wait()
        add_products(ids_ref, normed_ref, held.at[k], slot, parts)
    out_keep[...] = parts[0]
    out_send[...] = parts[1]


def project(ids, normed, slots, pieces, earlier=()):
    part = jax.ShapeDtypeStruct((normed.shape[2], 2 * HD), jnp.float32)
    return pl.pallas_call(
        functools.partial(project_kernel, slots, bool(earlier)),
        out_shape=(part, part),
        in_specs=[SMEM, VMEM] + [ANY] * len(pieces) + [VMEM] * len(earlier),
        out_specs=(VMEM, VMEM),
        scratch_shapes=[
            pltpu.VMEM((len(pieces),) + pieces[0].shape, pieces[0].dtype),
            pltpu.SemaphoreType.DMA((len(pieces),)),
        ],
        compiler_params=params(),
    )(ids, normed, *pieces, *earlier)


def join_kernel(mine_ref, theirs_ref, out_ref):
    rows = mine_ref.shape[0]
    total = (mine_ref[...] + theirs_ref[...]).astype(jnp.bfloat16)
    out_ref[0:rows, :] = total[:, 0:HD]
    for b in range(rows // HD):
        out_ref[rows + b * HD : rows + (b + 1) * HD, :] = jnp.transpose(
            total[b * HD : (b + 1) * HD, HD : 2 * HD]
        )


def attend_kernel(later, ids_ref, visible_ref, counts_ref, q_ref, kv0, kv1, kv2, kv3, out_ref, q_t, stat, acc):
    span_len = q_ref.shape[0]
    factor = LOG2E * HD ** (-0.5)
    quad = ids_ref[YH]

    @pl.when(quad + later < QUAD)
    def _():
        q_span = (quad + later) * QUAD + ids_ref[PLACE]
        q_t[...] = jnp.transpose(q_ref[...])
        stat[0:1, :] = jnp.full((1, span_len), NEG_BIG, jnp.float32)
        stat[8:9, :] = jnp.zeros((1, span_len), jnp.float32)
        acc[...] = jnp.zeros_like(acc)
        for flip, kv_ref in enumerate((kv0, kv1, kv2, kv3)):
            k_span = quad * QUAD + (ids_ref[PLACE] ^ flip)
            seen = visible_ref[q_span, k_span] == 1
            if later == 0:
                seen = (k_span == q_span) if flip == 0 else jnp.logical_and(seen, k_span < q_span)

            @pl.when(seen)
            def _():
                scores = jnp.dot(kv_ref[0:span_len, :], q_t[...], preferred_element_type=jnp.float32)
                live = lax.broadcasted_iota(jnp.int32, scores.shape, 0) < counts_ref[k_span]
                scores = jnp.where(live, scores * factor, NEG_BIG)
                best = stat[0:1, :]
                top = jnp.maximum(best, jnp.max(scores, axis=0, keepdims=True))
                weights = jnp.exp2(scores - top)
                fading = jnp.exp2(best - top)
                stat[8:9, :] = stat[8:9, :] * fading + jnp.sum(weights, axis=0, keepdims=True)
                stat[0:1, :] = top
                values = jnp.concatenate(
                    [kv_ref[span_len + b * HD : span_len + (b + 1) * HD, :] for b in range(span_len // HD)],
                    axis=1,
                )
                acc[...] = acc[...] * fading + jnp.dot(
                    values, weights.astype(jnp.bfloat16), preferred_element_type=jnp.float32
                )

        out_ref[0:HD, :] = acc[...].astype(jnp.bfloat16)
        rows = []
        for value in (stat[0:1, :], stat[8:9, :]):
            for _part in range(3):
                part = value.astype(jnp.bfloat16).astype(jnp.float32)
                rows.append(part)
                value = value - part
        rows.append(jnp.zeros((STAT_ROWS - 6, span_len), jnp.float32))
        out_ref[HD : HD + STAT_ROWS, :] = jnp.concatenate(rows, axis=0).astype(jnp.bfloat16)

    @pl.when(quad + later >= QUAD)
    def _():
        out_ref[...] = jnp.zeros_like(out_ref)


def attend(later, ids, visible, counts, q, kvs):
    span_len = q.shape[0]
    return pl.pallas_call(
        functools.partial(attend_kernel, later),
        out_shape=jax.ShapeDtypeStruct((HD + STAT_ROWS, span_len), jnp.bfloat16),
        in_specs=[SMEM] * 3 + [VMEM] * 5,
        out_specs=VMEM,
        scratch_shapes=[
            pltpu.VMEM((HD, span_len), jnp.bfloat16),
            pltpu.VMEM((16, span_len), jnp.float32),
            pltpu.VMEM((HD, span_len), jnp.float32),
        ],
        compiler_params=params(16),
    )(ids, visible, counts, q, *kvs)


def merge_kernel(ids_ref, counts_ref, part0, part1, part2, part3, out_ref):
    span_len = out_ref.shape[0]
    parts = (part0, part1, part2, part3)
    bests, totals = [], []
    for earlier, part in enumerate(parts):
        stat = part[HD : HD + STAT_ROWS, :].astype(jnp.float32)
        sent = ids_ref[YH] >= earlier
        bests.append(jnp.where(sent, (stat[0:1] + stat[1:2]) + stat[2:3], NEG_BIG))
        totals.append(jnp.where(sent, (stat[3:4] + stat[4:5]) + stat[5:6], 0.0))
    top = functools.reduce(jnp.maximum, bests)
    share = [jnp.exp2(b - top) for b in bests]
    total = sum(s * t for s, t in zip(share, totals))
    result = sum(s * part[0:HD, :].astype(jnp.float32) for s, part in zip(share, parts))
    slot = lax.broadcasted_iota(jnp.int32, total.shape, 1)
    result = jnp.where(slot < counts_ref[ids_ref[SPAN]], result / total, 0.0)
    out_ref[...] = jnp.transpose(result).astype(jnp.bfloat16)


def on_device(tokens, queries, key_weight, value_weight, modulation, levels, visible, counts):
    span_id = lax.axis_index(SPAN_AXES)
    ids = jnp.stack(
        [
            span_id,
            lax.axis_index("yh"),
            lax.axis_index(("yl", "xl")),
            lax.axis_index(("yh", "yl")),
            lax.axis_index("xl"),
            lax.axis_index("xh"),
            lax.axis_index("z"),
            lax.axis_index("c"),
        ]
    ).astype(jnp.int32)
    span_len, feats = tokens.shape
    depth = key_weight.shape[0] // 2

    w_type = jax.ShapeDtypeStruct((depth, 2 * HD), jnp.bfloat16)
    w_own, w_other = pl.pallas_call(
        split_kernel,
        out_shape=(w_type, w_type),
        in_specs=[SMEM, VMEM, VMEM],
        out_specs=(VMEM, VMEM),
        compiler_params=params(8),
    )(ids, key_weight, value_weight)
    w_chip = jnp.stack([w_own, shifted(w_other, "c", 2, 1)])
    w0 = jnp.concatenate([w_chip, shifted(w_chip, "xl", 2, 1)], axis=0)

    a0 = jnp.transpose(tokens)
    x0 = jnp.concatenate([a0, shifted(a0, "xh", 2, 1)], axis=0)

    x_up, x_down, w_up, w_down = [x0], [x0], [w0], [w0]
    y_axes = ("yh", "yl")
    for step in range(4):
        x_up.append(shifted(x_up[-1], "z", RING, 1))
        if step < 3:
            w_up.append(shifted(w_up[-1], y_axes, RING, 1))
            x_down.append(shifted(x_down[-1], "z", RING, -1))
        w_down.append(shifted(w_down[-1], y_axes, RING, -1))
    x_slots = [x0, x_down[1], x_down[2], x_down[3], x_up[4], x_up[3], x_up[2], x_up[1]]
    w_slots = [w0, w_down[1], w_down[2], w_down[3], w_down[4], w_up[3], w_up[2], w_up[1]]

    early = row_sums(x_slots[:4] + x_slots[5:])
    own_sums = row_sums([x_slots[4]], early)
    other_sums = shifted(own_sums, "c", 2, 1)
    mod_row = lax.dynamic_index_in_dim(modulation, levels[span_id], 0, keepdims=False)
    table = mod_row.astype(jnp.float32).reshape(-1, feats)
    normed = pl.pallas_call(
        norm_kernel,
        out_shape=jax.ShapeDtypeStruct((RING, 2, span_len, feats), jnp.bfloat16),
        in_specs=[SMEM] + [VMEM] * 3 + [ANY] * RING,
        out_specs=VMEM,
        scratch_shapes=[
            pltpu.VMEM((RING, 2 * feats, span_len), jnp.bfloat16),
            pltpu.SemaphoreType.DMA((RING,)),
        ],
        compiler_params=params(),
    )(ids, own_sums, other_sums, table, *x_slots)
    first = (0, 1, 2, 3, 5, 6, 7)
    parts = project(ids, normed, first, [w_slots[s] for s in first])
    mine, theirs = project(ids, normed, (4,), [w_slots[4]], parts)
    kv0 = pl.pallas_call(
        join_kernel,
        out_shape=jax.ShapeDtypeStruct((2 * span_len, HD), jnp.bfloat16),
        in_specs=[VMEM, VMEM],
        out_specs=VMEM,
        compiler_params=params(),
    )(mine, shifted(theirs, "c", 2, 1))

    kv1 = shifted(kv0, "xl", 2, 1)
    kv2 = shifted(kv0, "yl", 2, 1)
    kv3 = lax.ppermute(kv0, ("yl", "xl"), [(i, 3 - i) for i in range(4)])
    kvs = (kv0, kv1, kv2, kv3)
    parts = [None] * QUAD
    for later in (3, 2, 1, 0):
        q = moved(queries, -later) if later else queries
        part = attend(later, ids, visible, counts, q, kvs)
        parts[later] = moved(part, later) if later else part
    return pl.pallas_call(
        merge_kernel,
        out_shape=jax.ShapeDtypeStruct((span_len, HD), jnp.bfloat16),
        in_specs=[SMEM, SMEM] + [VMEM] * QUAD,
        out_specs=VMEM,
        compiler_params=params(8),
    )(ids, counts, *parts)


def solution(mesh):
    fine = Mesh(mesh.devices.reshape(SIZES), SPAN_AXES + FSDP_AXES)
    spread = P(SPAN_AXES, FSDP_AXES)
    return jax.shard_map(
        on_device,
        mesh=fine,
        in_specs=(spread, spread, spread, spread, P(), P(), P(), P()),
        out_specs=spread,
        check_vma=False,
    )
```

```python
import functools

import jax
import jax.numpy as jnp
from jax import lax
from jax.experimental import pallas as pl
from jax.experimental.pallas import tpu as pltpu
from jax.sharding import Mesh, PartitionSpec as P

HD = 128
EPSILON = 1e-06
NEG_BIG = -1e30
LOG2E = 1.4426950408889634
SPAN_AXES = ("yh", "yl", "xl")
FSDP_AXES = ("xh", "z", "c")
SIZES = (4, 2, 2, 2, 8, 2)
QUAD = 4
RING = 8
STAT_ROWS = 16
SPAN, YH, PLACE, Y, XL, XH, Z, CORE, LEVEL = range(9)

VMEM = pl.BlockSpec(memory_space=pltpu.VMEM)
SMEM = pl.BlockSpec(memory_space=pltpu.SMEM)
HBM = pl.BlockSpec(memory_space=pltpu.HBM)


def params(mib=12):
    return pltpu.CompilerParams(vmem_limit_bytes=mib * 1024 * 1024)


def shifted(value, axis, size, by):
    return lax.ppermute(value, axis, [(i, (i + by) % size) for i in range(size)])


def moved(value, by):
    return lax.ppermute(value, "yh", [(i, i + by) for i in range(QUAD) if 0 <= i + by < QUAD])


def split_kernel(ids_ref, key_ref, value_ref, own_ref, other_ref, sems):
    rows = own_ref.shape[0]
    copies = []
    for part, out in ((1 - ids_ref[CORE], other_ref), (ids_ref[CORE], own_ref)):
        first = pl.multiple_of(part * rows, 16)
        for column, ref in enumerate((key_ref, value_ref)):
            copies.append(
                pltpu.make_async_copy(
                    ref.at[pl.ds(first, rows), :],
                    out.at[:, pl.ds(column * HD, HD)],
                    sems.at[len(copies)],
                )
            )
    for copy in copies:
        copy.start()
    for copy in copies:
        copy.wait()


def table_kernel(levels_ref, ids_ref, modulation_ref, out_ref):
    feats = out_ref.shape[1]
    rows = modulation_ref[...].astype(jnp.float32)
    chosen = lax.broadcasted_iota(jnp.int32, rows.shape, 0) == levels_ref[ids_ref[SPAN]]
    row = jnp.sum(jnp.where(chosen, rows, 0.0), axis=0, keepdims=True)
    for block in range(out_ref.shape[0]):
        out_ref[block : block + 1, :] = row[:, block * feats : (block + 1) * feats]


def sums_kernel(count, has_earlier, *refs):
    out = refs[-1]
    total = jnp.zeros((1, out.shape[1]), jnp.float32)
    square = jnp.zeros((1, out.shape[1]), jnp.float32)
    for ref in refs[:count]:
        block = ref[...].astype(jnp.float32)
        total += jnp.sum(block, axis=0, keepdims=True)
        square += jnp.sum(block * block, axis=0, keepdims=True)
    if has_earlier:
        total += refs[count][0:1, :]
        square += refs[count][1:2, :]
    out[...] = jnp.zeros_like(out)
    out[0:1, :] = total
    out[1:2, :] = square


def row_sums(pieces, earlier=None):
    rest = () if earlier is None else (earlier,)
    return pl.pallas_call(
        functools.partial(sums_kernel, len(pieces), bool(rest)),
        out_shape=jax.ShapeDtypeStruct((8, pieces[0].shape[1]), jnp.float32),
        in_specs=[VMEM] * (len(pieces) + len(rest)),
        out_specs=VMEM,
        compiler_params=params(),
    )(*pieces, *rest)


def norm_kernel(ids_ref, own_ref, other_ref, table_ref, *refs):
    pieces, normed_ref = refs[:RING], refs[RING]
    feats = pieces[0].shape[0] // 2
    model_width = 4.0 * RING * feats
    stats = own_ref[...] + other_ref[...]
    mean = stats[0:1, :] / model_width
    variance = stats[1:2, :] / model_width - mean * mean
    rstd = lax.rsqrt(variance + EPSILON)
    columns = jnp.transpose(jnp.concatenate([mean, rstd, jnp.zeros((6, mean.shape[1]), jnp.float32)], axis=0))
    mean_col, rstd_col = columns[:, 0:1], columns[:, 1:2]
    blocks = table_ref.shape[0] // 2
    for slot, piece in enumerate(pieces):
        for part in range(2):
            x_at = jnp.where(part == 0, ids_ref[XH], 1 - ids_ref[XH])
            z_at = lax.rem(ids_ref[Z] + slot, RING)
            row = x_at * (2 * RING) + z_at * 2 + ids_ref[CORE]
            shift = table_ref[pl.ds(row, 1), :]
            scale = table_ref[pl.ds(blocks + row, 1), :]
            block = jnp.transpose(piece[part * feats : (part + 1) * feats, :]).astype(jnp.float32)
            block = (block - mean_col) * rstd_col * (1.0 + scale) + shift
            normed_ref[slot, part] = block.astype(jnp.bfloat16)


def add_products(ids_ref, normed_ref, weights, slot, parts):
    y_at = lax.rem(ids_ref[Y] + slot, RING)
    half = y_at // (RING // 2)
    part = jnp.where(half == ids_ref[XH], 0, 1)
    for head in range(2):
        for side in range(2):
            xl_at = ids_ref[XL] if side == 0 else 1 - ids_ref[XL]
            z_at = 2 * (y_at - half * (RING // 2)) + xl_at
            place = lax.rem(z_at + RING - ids_ref[Z], RING)
            product = jnp.dot(normed_ref[place, part], weights[2 * side + head], preferred_element_type=jnp.float32)
            parts[head] = product if parts[head] is None else parts[head] + product


def project_kernel(slots, has_earlier, ids_ref, normed_ref, *refs):
    pieces = refs[: len(slots)]
    out_keep, out_send = refs[-2:]
    if has_earlier:
        parts = [refs[len(slots)][...], refs[len(slots) + 1][...]]
    else:
        parts = [None, None]
    for k, slot in enumerate(slots):
        add_products(ids_ref, normed_ref, pieces[k], slot, parts)
    out_keep[...] = parts[0]
    out_send[...] = parts[1]


def project(ids, normed, slots, pieces, earlier=()):
    part = jax.ShapeDtypeStruct((normed.shape[2], 2 * HD), jnp.float32)
    return pl.pallas_call(
        functools.partial(project_kernel, slots, bool(earlier)),
        out_shape=(part, part),
        in_specs=[SMEM, VMEM] + [VMEM] * (len(pieces) + len(earlier)),
        out_specs=(VMEM, VMEM),
        compiler_params=params(),
    )(ids, normed, *pieces, *earlier)


def join_kernel(mine_ref, theirs_ref, out_ref):
    rows = mine_ref.shape[0]
    total = (mine_ref[...] + theirs_ref[...]).astype(jnp.bfloat16)
    out_ref[0:rows, :] = total[:, 0:HD]
    for b in range(rows // HD):
        out_ref[rows + b * HD : rows + (b + 1) * HD, :] = jnp.transpose(
            total[b * HD : (b + 1) * HD, HD : 2 * HD]
        )


def scan_keys(later, flips, ids_ref, visible_ref, counts_ref, q_t, kv_refs, stat, acc):
    factor = LOG2E * HD ** (-0.5)
    quad, place = ids_ref[YH], ids_ref[PLACE]
    q_span = jnp.minimum((quad + later) * QUAD + place, QUAD * QUAD - 1)
    for flip, kv_ref in zip(flips, kv_refs):
        k_span = quad * QUAD + (place ^ flip)
        span_len = kv_ref.shape[0] // 2
        seen = visible_ref[q_span, k_span] == 1
        if later == 0:
            seen = (k_span == q_span) if flip == 0 else jnp.logical_and(seen, k_span < q_span)
        else:
            seen = jnp.logical_and(seen, quad + later < QUAD)

        @pl.when(seen)
        def _():
            scores = jnp.dot(kv_ref[0:span_len, :], q_t[...], preferred_element_type=jnp.float32)
            live = lax.broadcasted_iota(jnp.int32, scores.shape, 0) < counts_ref[k_span]
            scores = jnp.where(live, scores * factor, NEG_BIG)
            best = stat[0:1, :]
            top = jnp.maximum(best, jnp.max(scores, axis=0, keepdims=True))
            weights = jnp.exp2(scores - top)
            fading = jnp.exp2(best - top)
            stat[8:9, :] = stat[8:9, :] * fading + jnp.sum(weights, axis=0, keepdims=True)
            stat[0:1, :] = top
            values = jnp.concatenate(
                [kv_ref[span_len + b * HD : span_len + (b + 1) * HD, :] for b in range(span_len // HD)], axis=1
            )
            acc[...] = acc[...] * fading + jnp.dot(
                values, weights.astype(jnp.bfloat16), preferred_element_type=jnp.float32
            )


def begin_kernel(ids_ref, visible_ref, counts_ref, q0, q1, q2, q3, kv_ref, q_t, stat, acc):
    for later, q_ref in enumerate((q0, q1, q2, q3)):
        q_t[later] = jnp.transpose(q_ref[...])
        stat[later, 0:8, :] = jnp.full((8, stat.shape[2]), NEG_BIG, jnp.float32)
        stat[later, 8:16, :] = jnp.zeros((8, stat.shape[2]), jnp.float32)
        acc[later] = jnp.zeros(acc.shape[1:], jnp.float32)
        scan_keys(
            later, (0,), ids_ref, visible_ref, counts_ref, q_t.at[later], (kv_ref,), stat.at[later], acc.at[later]
        )


def middle_kernel(ids_ref, visible_ref, counts_ref, q_t, stat_in, acc_in, kv_ref, stat, acc):
    for later in range(QUAD):
        scan_keys(
            later, (1,), ids_ref, visible_ref, counts_ref, q_t.at[later], (kv_ref,), stat.at[later], acc.at[later]
        )


def finish_kernel(later, ids_ref, visible_ref, counts_ref, q_t, stat_in, acc_in, kv2, kv3, out_ref, stat, acc):
    span_len = out_ref.shape[1]

    @pl.when(ids_ref[YH] + later < QUAD)
    def _():
        stat[...] = stat_in[later]
        acc[...] = acc_in[later]
        scan_keys(later, (2, 3), ids_ref, visible_ref, counts_ref, q_t.at[later], (kv2, kv3), stat, acc)
        out_ref[0:HD, :] = acc[...].astype(jnp.bfloat16)
        rows = []
        for value in (stat[0:1, :], stat[8:9, :]):
            for _part in range(3):
                part = value.astype(jnp.bfloat16).astype(jnp.float32)
                rows.append(part)
                value = value - part
        rows.append(jnp.zeros((STAT_ROWS - 6, span_len), jnp.float32))
        out_ref[HD : HD + STAT_ROWS, :] = jnp.concatenate(rows, axis=0).astype(jnp.bfloat16)

    @pl.when(ids_ref[YH] + later >= QUAD)
    def _():
        out_ref[...] = jnp.zeros_like(out_ref)


def merge_kernel(ids_ref, counts_ref, part0, part1, part2, part3, out_ref):
    span_len = out_ref.shape[0]
    parts = (part0, part1, part2, part3)
    bests, totals = [], []
    for earlier, part in enumerate(parts):
        stat = part[HD : HD + STAT_ROWS, :].astype(jnp.float32)
        sent = ids_ref[YH] >= earlier
        bests.append(jnp.where(sent, (stat[0:1] + stat[1:2]) + stat[2:3], NEG_BIG))
        totals.append(jnp.where(sent, (stat[3:4] + stat[4:5]) + stat[5:6], 0.0))
    top = functools.reduce(jnp.maximum, bests)
    share = [jnp.exp2(b - top) for b in bests]
    total = sum(s * t for s, t in zip(share, totals))
    result = sum(s * part[0:HD, :].astype(jnp.float32) for s, part in zip(share, parts))
    slot = lax.broadcasted_iota(jnp.int32, total.shape, 1)
    result = jnp.where(slot < counts_ref[ids_ref[SPAN]], result / total, 0.0)
    out_ref[...] = jnp.transpose(result).astype(jnp.bfloat16)


def on_device(tokens, queries, key_weight, value_weight, modulation, levels, visible, counts):
    span_id = lax.axis_index(SPAN_AXES)
    ids = jnp.stack(
        [
            span_id,
            lax.axis_index("yh"),
            lax.axis_index(("yl", "xl")),
            lax.axis_index(("yh", "yl")),
            lax.axis_index("xl"),
            lax.axis_index("xh"),
            lax.axis_index("z"),
            lax.axis_index("c"),
        ]
    ).astype(jnp.int32)
    span_len, feats = tokens.shape
    depth = key_weight.shape[0] // 2

    w_type = jax.ShapeDtypeStruct((depth, 2 * HD), jnp.bfloat16)
    w_own, w_other = pl.pallas_call(
        split_kernel,
        out_shape=(w_type, w_type),
        in_specs=[SMEM, HBM, HBM],
        out_specs=(VMEM, VMEM),
        scratch_shapes=[pltpu.SemaphoreType.DMA((4,))],
        compiler_params=params(),
    )(ids, key_weight, value_weight)
    w_chip = jnp.stack([w_own, shifted(w_other, "c", 2, 1)])
    w0 = jnp.concatenate([w_chip, shifted(w_chip, "xl", 2, 1)], axis=0)

    a0 = jnp.transpose(tokens)
    x0 = jnp.concatenate([a0, shifted(a0, "xh", 2, 1)], axis=0)

    q_later = [moved(queries, -later) for later in (1, 2, 3)]
    w0, *q_later = lax.optimization_barrier((w0, *q_later))

    x_up, x_down, w_up, w_down = [x0], [x0], [w0], [w0]
    y_axes = ("yh", "yl")
    for step in range(4):
        x_up.append(shifted(x_up[-1], "z", RING, 1))
        if step < 3:
            w_up.append(shifted(w_up[-1], y_axes, RING, 1))
            x_down.append(shifted(x_down[-1], "z", RING, -1))
        w_down.append(shifted(w_down[-1], y_axes, RING, -1))
    x_slots = [x0, x_down[1], x_down[2], x_down[3], x_up[4], x_up[3], x_up[2], x_up[1]]
    w_slots = [w0, w_down[1], w_down[2], w_down[3], w_down[4], w_up[3], w_up[2], w_up[1]]

    early = row_sums(x_slots[:4] + x_slots[5:])
    own_sums = row_sums([x_slots[4]], early)
    other_sums = shifted(own_sums, "c", 2, 1)
    table = pl.pallas_call(
        table_kernel,
        out_shape=jax.ShapeDtypeStruct((modulation.shape[1] // feats, feats), jnp.float32),
        in_specs=[SMEM, SMEM, VMEM],
        out_specs=VMEM,
        compiler_params=params(),
    )(levels, ids, modulation)
    normed = pl.pallas_call(
        norm_kernel,
        out_shape=jax.ShapeDtypeStruct((RING, 2, span_len, feats), jnp.bfloat16),
        in_specs=[SMEM] + [VMEM] * (3 + RING),
        out_specs=VMEM,
        compiler_params=params(),
    )(ids, own_sums, other_sums, table, *x_slots)
    first = (0, 1, 2, 3, 5, 6, 7)
    parts = project(ids, normed, first, [w_slots[s] for s in first])
    mine, theirs = project(ids, normed, (4,), [w_slots[4]], parts)
    kv0 = pl.pallas_call(
        join_kernel,
        out_shape=jax.ShapeDtypeStruct((2 * span_len, HD), jnp.bfloat16),
        in_specs=[VMEM, VMEM],
        out_specs=VMEM,
        compiler_params=params(),
    )(mine, shifted(theirs, "c", 2, 1))

    kv1 = shifted(kv0, "xl", 2, 1)
    kv2 = shifted(kv0, "yl", 2, 1)
    kv3 = lax.ppermute(kv0, ("yl", "xl"), [(i, 3 - i) for i in range(4)])
    scalars = (ids, visible, counts)
    q_type = jax.ShapeDtypeStruct((QUAD, HD, span_len), jnp.bfloat16)
    stat_type = jax.ShapeDtypeStruct((QUAD, 16, span_len), jnp.float32)
    acc_type = jax.ShapeDtypeStruct((QUAD, HD, span_len), jnp.float32)
    q_t, stat, acc = pl.pallas_call(
        begin_kernel,
        out_shape=(q_type, stat_type, acc_type),
        in_specs=[SMEM] * 3 + [VMEM] * 5,
        out_specs=(VMEM,) * 3,
        compiler_params=params(),
    )(*scalars, queries, *q_later, kv0)
    stat, acc = pl.pallas_call(
        middle_kernel,
        out_shape=(stat_type, acc_type),
        in_specs=[SMEM] * 3 + [VMEM] * 4,
        out_specs=(VMEM,) * 2,
        input_output_aliases={4: 0, 5: 1},
        compiler_params=params(),
    )(*scalars, q_t, stat, acc, kv1)
    parts = [None] * QUAD
    for later in (3, 2, 1, 0):
        part = pl.pallas_call(
            functools.partial(finish_kernel, later),
            out_shape=jax.ShapeDtypeStruct((HD + STAT_ROWS, span_len), jnp.bfloat16),
            in_specs=[SMEM] * 3 + [VMEM] * 5,
            out_specs=VMEM,
            scratch_shapes=[pltpu.VMEM((16, span_len), jnp.float32), pltpu.VMEM((HD, span_len), jnp.float32)],
            compiler_params=params(),
        )(*scalars, q_t, stat, acc, kv2, kv3)
        parts[later] = moved(part, later) if later else part
    return pl.pallas_call(
        merge_kernel,
        out_shape=jax.ShapeDtypeStruct((span_len, HD), jnp.bfloat16),
        in_specs=[SMEM, SMEM] + [VMEM] * QUAD,
        out_specs=VMEM,
        compiler_params=params(),
    )(ids, counts, *parts)


def solution(mesh):
    fine = Mesh(mesh.devices.reshape(SIZES), SPAN_AXES + FSDP_AXES)
    spread = P(SPAN_AXES, FSDP_AXES)
    return jax.shard_map(
        on_device,
        mesh=fine,
        in_specs=(spread, spread, spread, spread, P(), P(), P(), P()),
        out_specs=spread,
        check_vma=False,
    )
```

```python
import functools

import jax
import jax.numpy as jnp
from jax import lax
from jax.experimental import pallas as pl
from jax.experimental.pallas import tpu as pltpu
from jax.sharding import Mesh, PartitionSpec as P

HD = 128
EPSILON = 1e-06
NEG_BIG = -1e30
LOG2E = 1.4426950408889634
SPAN_AXES = ("yh", "yl", "xl")
FSDP_AXES = ("xh", "z", "c")
SIZES = (4, 2, 2, 2, 8, 2)
QUAD = 4
RING = 8
STAT_ROWS = 16
SPAN, YH, PLACE, Y, XL, XH, Z, CORE, LEVEL = range(9)

VMEM = pl.BlockSpec(memory_space=pltpu.VMEM)
SMEM = pl.BlockSpec(memory_space=pltpu.SMEM)


def params(mib=12):
    return pltpu.CompilerParams(vmem_limit_bytes=mib * 1024 * 1024)


def shifted(value, axis, size, by):
    return lax.ppermute(value, axis, [(i, (i + by) % size) for i in range(size)])


def turned(place, later):
    return place ^ 2 if later == 2 else place


def moved(value, by):
    pairs = []
    for yh in range(QUAD):
        for yl in range(2):
            if 0 <= yh + by < QUAD:
                pairs.append((2 * yh + yl, 2 * (yh + by) + turned(2 * yl, abs(by)) // 2))
    return lax.ppermute(value, ("yh", "yl"), pairs)


def split_kernel(ids_ref, key_ref, value_ref, own_ref, other_ref):
    rows = own_ref.shape[0]
    for part, out in ((ids_ref[CORE], own_ref), (1 - ids_ref[CORE], other_ref)):
        first = pl.multiple_of(part * rows, 16)
        out[:, 0:HD] = key_ref[pl.ds(first, rows), :]
        out[:, HD : 2 * HD] = value_ref[pl.ds(first, rows), :]


def table_kernel(levels_ref, ids_ref, modulation_ref, out_ref):
    feats = out_ref.shape[1]
    rows = modulation_ref[...].astype(jnp.float32)
    chosen = lax.broadcasted_iota(jnp.int32, rows.shape, 0) == levels_ref[ids_ref[SPAN]]
    row = jnp.sum(jnp.where(chosen, rows, 0.0), axis=0, keepdims=True)
    for block in range(out_ref.shape[0]):
        out_ref[block : block + 1, :] = row[:, block * feats : (block + 1) * feats]


def sums_kernel(count, has_earlier, *refs):
    out = refs[-1]
    total = jnp.zeros((1, out.shape[1]), jnp.float32)
    square = jnp.zeros((1, out.shape[1]), jnp.float32)
    for ref in refs[:count]:
        block = ref[...].astype(jnp.float32)
        total += jnp.sum(block, axis=0, keepdims=True)
        square += jnp.sum(block * block, axis=0, keepdims=True)
    if has_earlier:
        total += refs[count][0:1, :]
        square += refs[count][1:2, :]
    out[...] = jnp.zeros_like(out)
    out[0:1, :] = total
    out[1:2, :] = square


def row_sums(pieces, earlier=None):
    rest = () if earlier is None else (earlier,)
    return pl.pallas_call(
        functools.partial(sums_kernel, len(pieces), bool(rest)),
        out_shape=jax.ShapeDtypeStruct((8, pieces[0].shape[1]), jnp.float32),
        in_specs=[VMEM] * (len(pieces) + len(rest)),
        out_specs=VMEM,
        compiler_params=params(),
    )(*pieces, *rest)


def norm_kernel(ids_ref, own_ref, other_ref, table_ref, *refs):
    pieces, normed_ref = refs[:RING], refs[RING]
    feats = pieces[0].shape[0] // 2
    model_width = 4.0 * RING * feats
    stats = own_ref[...] + other_ref[...]
    mean = stats[0:1, :] / model_width
    variance = stats[1:2, :] / model_width - mean * mean
    rstd = lax.rsqrt(variance + EPSILON)
    columns = jnp.transpose(jnp.concatenate([mean, rstd, jnp.zeros((6, mean.shape[1]), jnp.float32)], axis=0))
    mean_col, rstd_col = columns[:, 0:1], columns[:, 1:2]
    blocks = table_ref.shape[0] // 2
    for slot, piece in enumerate(pieces):
        for part in range(2):
            x_at = jnp.where(part == 0, ids_ref[XH], 1 - ids_ref[XH])
            z_at = lax.rem(ids_ref[Z] + slot, RING)
            row = x_at * (2 * RING) + z_at * 2 + ids_ref[CORE]
            shift = table_ref[pl.ds(row, 1), :]
            scale = table_ref[pl.ds(blocks + row, 1), :]
            block = jnp.transpose(piece[part * feats : (part + 1) * feats, :]).astype(jnp.float32)
            block = (block - mean_col) * rstd_col * (1.0 + scale) + shift
            normed_ref[slot, part] = block.astype(jnp.bfloat16)


def project_kernel(head, ids_ref, normed_ref, *refs):
    pieces, out_ref = refs[:RING], refs[RING]
    for slot, weights in enumerate(pieces):
        y_at = lax.rem(ids_ref[Y] + slot, RING)
        half = y_at // (RING // 2)
        part = jnp.where(half == ids_ref[XH], 0, 1)
        product = None
        for side in range(2):
            xl_at = ids_ref[XL] if side == 0 else 1 - ids_ref[XL]
            z_at = 2 * (y_at - half * (RING // 2)) + xl_at
            place = lax.rem(z_at + RING - ids_ref[Z], RING)
            term = jnp.dot(normed_ref[place, part], weights[2 * side + head], preferred_element_type=jnp.float32)
            product = term if product is None else product + term
        if slot == 0:
            out_ref[...] = product
        else:
            out_ref[...] += product


def project(head, ids, normed, pieces):
    return pl.pallas_call(
        functools.partial(project_kernel, head),
        out_shape=jax.ShapeDtypeStruct((normed.shape[2], 2 * HD), jnp.float32),
        in_specs=[SMEM] + [VMEM] * (1 + RING),
        out_specs=VMEM,
        compiler_params=params(),
    )(ids, normed, *pieces)


def join_kernel(mine_ref, theirs_ref, out_ref):
    rows = mine_ref.shape[0]
    total = (mine_ref[...] + theirs_ref[...]).astype(jnp.bfloat16)
    out_ref[0:rows, :] = total[:, 0:HD]
    for b in range(rows // HD):
        out_ref[rows + b * HD : rows + (b + 1) * HD, :] = jnp.transpose(
            total[b * HD : (b + 1) * HD, HD : 2 * HD]
        )


def scan_keys(later, flips, ids_ref, visible_ref, counts_ref, q_t, kv_refs, stat, acc):
    factor = LOG2E * HD ** (-0.5)
    quad, place = ids_ref[YH], ids_ref[PLACE]
    q_span = jnp.minimum((quad + later) * QUAD + turned(place, later), QUAD * QUAD - 1)
    for flip, kv_ref in zip(flips, kv_refs):
        k_span = quad * QUAD + (place ^ flip)
        span_len = kv_ref.shape[0] // 2
        seen = visible_ref[q_span, k_span] == 1
        if later == 0:
            seen = (k_span == q_span) if flip == 0 else jnp.logical_and(seen, k_span < q_span)
        else:
            seen = jnp.logical_and(seen, quad + later < QUAD)

        @pl.when(seen)
        def _():
            scores = jnp.dot(kv_ref[0:span_len, :], q_t[...], preferred_element_type=jnp.float32)
            live = lax.broadcasted_iota(jnp.int32, scores.shape, 0) < counts_ref[k_span]
            scores = jnp.where(live, scores * factor, NEG_BIG)
            best = stat[0:1, :]
            top = jnp.maximum(best, jnp.max(scores, axis=0, keepdims=True))
            weights = jnp.exp2(scores - top)
            fading = jnp.exp2(best - top)
            stat[8:9, :] = stat[8:9, :] * fading + jnp.sum(weights, axis=0, keepdims=True)
            stat[0:1, :] = top
            values = jnp.concatenate(
                [kv_ref[span_len + b * HD : span_len + (b + 1) * HD, :] for b in range(span_len // HD)], axis=1
            )
            acc[...] = acc[...] * fading + jnp.dot(
                values, weights.astype(jnp.bfloat16), preferred_element_type=jnp.float32
            )


def begin_kernel(ids_ref, visible_ref, counts_ref, q0, q1, q2, q3, kv_ref, q_t, stat, acc):
    for later, q_ref in enumerate((q0, q1, q2, q3)):
        q_t[later] = jnp.transpose(q_ref[...])
        stat[later, 0:8, :] = jnp.full((8, stat.shape[2]), NEG_BIG, jnp.float32)
        stat[later, 8:16, :] = jnp.zeros((8, stat.shape[2]), jnp.float32)
        acc[later] = jnp.zeros(acc.shape[1:], jnp.float32)
        scan_keys(
            later, (0,), ids_ref, visible_ref, counts_ref, q_t.at[later], (kv_ref,), stat.at[later], acc.at[later]
        )


def middle_kernel(ids_ref, visible_ref, counts_ref, q_t, stat_in, acc_in, kv_ref, stat, acc):
    for later in range(QUAD):
        scan_keys(
            later, (2,), ids_ref, visible_ref, counts_ref, q_t.at[later], (kv_ref,), stat.at[later], acc.at[later]
        )


def finish_kernel(later, ids_ref, visible_ref, counts_ref, q_t, stat_in, acc_in, kv1, kv3, out_ref, stat, acc):
    span_len = out_ref.shape[1]

    @pl.when(ids_ref[YH] + later < QUAD)
    def _():
        stat[...] = stat_in[later]
        acc[...] = acc_in[later]
        scan_keys(later, (1, 3), ids_ref, visible_ref, counts_ref, q_t.at[later], (kv1, kv3), stat, acc)
        out_ref[0:HD, :] = acc[...].astype(jnp.bfloat16)
        rows = []
        for value in (stat[0:1, :], stat[8:9, :]):
            for _part in range(3):
                part = value.astype(jnp.bfloat16).astype(jnp.float32)
                rows.append(part)
                value = value - part
        rows.append(jnp.zeros((STAT_ROWS - 6, span_len), jnp.float32))
        out_ref[HD : HD + STAT_ROWS, :] = jnp.concatenate(rows, axis=0).astype(jnp.bfloat16)

    @pl.when(ids_ref[YH] + later >= QUAD)
    def _():
        out_ref[...] = jnp.zeros_like(out_ref)


def merge_kernel(ids_ref, counts_ref, part0, part1, part2, part3, out_ref):
    span_len = out_ref.shape[0]
    parts = (part0, part1, part2, part3)
    bests, totals = [], []
    for earlier, part in enumerate(parts):
        stat = part[HD : HD + STAT_ROWS, :].astype(jnp.float32)
        sent = ids_ref[YH] >= earlier
        bests.append(jnp.where(sent, (stat[0:1] + stat[1:2]) + stat[2:3], NEG_BIG))
        totals.append(jnp.where(sent, (stat[3:4] + stat[4:5]) + stat[5:6], 0.0))
    top = functools.reduce(jnp.maximum, bests)
    share = [jnp.exp2(b - top) for b in bests]
    total = sum(s * t for s, t in zip(share, totals))
    result = sum(s * part[0:HD, :].astype(jnp.float32) for s, part in zip(share, parts))
    slot = lax.broadcasted_iota(jnp.int32, total.shape, 1)
    result = jnp.where(slot < counts_ref[ids_ref[SPAN]], result / total, 0.0)
    out_ref[...] = jnp.transpose(result).astype(jnp.bfloat16)


def on_device(tokens, queries, key_weight, value_weight, modulation, levels, visible, counts):
    span_id = lax.axis_index(SPAN_AXES)
    ids = jnp.stack(
        [
            span_id,
            lax.axis_index("yh"),
            lax.axis_index(("yl", "xl")),
            lax.axis_index(("yh", "yl")),
            lax.axis_index("xl"),
            lax.axis_index("xh"),
            lax.axis_index("z"),
            lax.axis_index("c"),
        ]
    ).astype(jnp.int32)
    span_len, feats = tokens.shape
    depth = key_weight.shape[0] // 2

    w_type = jax.ShapeDtypeStruct((depth, 2 * HD), jnp.bfloat16)
    w_own, w_other = pl.pallas_call(
        split_kernel,
        out_shape=(w_type, w_type),
        in_specs=[SMEM, VMEM, VMEM],
        out_specs=(VMEM, VMEM),
        compiler_params=params(),
    )(ids, key_weight, value_weight)
    w_chip = jnp.stack([w_own, shifted(w_other, "c", 2, 1)])
    w0 = jnp.concatenate([w_chip, shifted(w_chip, "xl", 2, 1)], axis=0)

    a0 = jnp.transpose(tokens)
    x0 = jnp.concatenate([a0, shifted(a0, "xh", 2, 1)], axis=0)

    q_later = [moved(queries, -later) for later in (1, 2, 3)]
    w0, *q_later = lax.optimization_barrier((w0, *q_later))

    x_up, x_down, w_up, w_down = [x0], [x0], [w0], [w0]
    y_axes = ("yh", "yl")
    for step in range(4):
        x_up.append(shifted(x_up[-1], "z", RING, 1))
        if step < 3:
            w_up.append(shifted(w_up[-1], y_axes, RING, 1))
            x_down.append(shifted(x_down[-1], "z", RING, -1))
        w_down.append(shifted(w_down[-1], y_axes, RING, -1))
    x_slots = [x0, x_down[1], x_down[2], x_down[3], x_up[4], x_up[3], x_up[2], x_up[1]]
    w_slots = [w0, w_down[1], w_down[2], w_down[3], w_down[4], w_up[3], w_up[2], w_up[1]]

    early = row_sums(x_slots[:4] + x_slots[5:])
    own_sums = row_sums([x_slots[4]], early)
    other_sums = shifted(own_sums, "c", 2, 1)
    table = pl.pallas_call(
        table_kernel,
        out_shape=jax.ShapeDtypeStruct((modulation.shape[1] // feats, feats), jnp.float32),
        in_specs=[SMEM, SMEM, VMEM],
        out_specs=VMEM,
        compiler_params=params(),
    )(levels, ids, modulation)
    normed = pl.pallas_call(
        norm_kernel,
        out_shape=jax.ShapeDtypeStruct((RING, 2, span_len, feats), jnp.bfloat16),
        in_specs=[SMEM] + [VMEM] * (3 + RING),
        out_specs=VMEM,
        compiler_params=params(),
    )(ids, own_sums, other_sums, table, *x_slots)
    theirs = shifted(project(1, ids, normed, w_slots), "c", 2, 1)
    mine = project(0, ids, normed, w_slots)
    kv0 = pl.pallas_call(
        join_kernel,
        out_shape=jax.ShapeDtypeStruct((2 * span_len, HD), jnp.bfloat16),
        in_specs=[VMEM, VMEM],
        out_specs=VMEM,
        compiler_params=params(),
    )(mine, theirs)

    kv1 = shifted(kv0, "xl", 2, 1)
    kv2 = shifted(kv0, "yl", 2, 1)
    kv3 = lax.ppermute(kv0, ("yl", "xl"), [(i, 3 - i) for i in range(4)])
    scalars = (ids, visible, counts)
    q_type = jax.ShapeDtypeStruct((QUAD, HD, span_len), jnp.bfloat16)
    stat_type = jax.ShapeDtypeStruct((QUAD, 16, span_len), jnp.float32)
    acc_type = jax.ShapeDtypeStruct((QUAD, HD, span_len), jnp.float32)
    q_t, stat, acc = pl.pallas_call(
        begin_kernel,
        out_shape=(q_type, stat_type, acc_type),
        in_specs=[SMEM] * 3 + [VMEM] * 5,
        out_specs=(VMEM,) * 3,
        compiler_params=params(),
    )(*scalars, queries, *q_later, kv0)
    stat, acc = pl.pallas_call(
        middle_kernel,
        out_shape=(stat_type, acc_type),
        in_specs=[SMEM] * 3 + [VMEM] * 4,
        out_specs=(VMEM,) * 2,
        input_output_aliases={4: 0, 5: 1},
        compiler_params=params(),
    )(*scalars, q_t, stat, acc, kv2)
    parts = [None] * QUAD
    for later in (2, 3, 1, 0):
        part = pl.pallas_call(
            functools.partial(finish_kernel, later),
            out_shape=jax.ShapeDtypeStruct((HD + STAT_ROWS, span_len), jnp.bfloat16),
            in_specs=[SMEM] * 3 + [VMEM] * 5,
            out_specs=VMEM,
            scratch_shapes=[pltpu.VMEM((16, span_len), jnp.float32), pltpu.VMEM((HD, span_len), jnp.float32)],
            compiler_params=params(),
        )(*scalars, q_t, stat, acc, kv1, kv3)
        parts[later] = moved(part, later) if later else part
    return pl.pallas_call(
        merge_kernel,
        out_shape=jax.ShapeDtypeStruct((span_len, HD), jnp.bfloat16),
        in_specs=[SMEM, SMEM] + [VMEM] * QUAD,
        out_specs=VMEM,
        compiler_params=params(),
    )(ids, counts, *parts)


def solution(mesh):
    fine = Mesh(mesh.devices.reshape(SIZES), SPAN_AXES + FSDP_AXES)
    spread = P(SPAN_AXES, FSDP_AXES)
    return jax.shard_map(
        on_device,
        mesh=fine,
        in_specs=(spread, spread, spread, spread, P(), P(), P(), P()),
        out_specs=spread,
        check_vma=False,
    )
```

```python
import functools

import jax
import jax.numpy as jnp
from jax import lax
from jax.experimental import pallas as pl
from jax.experimental.pallas import tpu as pltpu
from jax.sharding import Mesh, PartitionSpec as P

HD = 128
EPSILON = 1e-06
NEG_BIG = -1e30
LOG2E = 1.4426950408889634
SPAN_AXES = ("yh", "yl", "xl")
FSDP_AXES = ("xh", "z", "c")
SIZES = (4, 2, 2, 2, 8, 2)
QUAD = 4
RING = 8
STAT_ROWS = 16
SPAN, YH, PLACE, Y, XL, XH, Z, CORE, LEVEL = range(9)

VMEM = pl.BlockSpec(memory_space=pltpu.VMEM)
SMEM = pl.BlockSpec(memory_space=pltpu.SMEM)


def params(mib=12):
    return pltpu.CompilerParams(vmem_limit_bytes=mib * 1024 * 1024)


def shifted(value, axis, size, by):
    return lax.ppermute(value, axis, [(i, (i + by) % size) for i in range(size)])


def turned(place, later):
    return place ^ 2 if later == 2 else place


def moved(value, by):
    pairs = []
    for yh in range(QUAD):
        for yl in range(2):
            if 0 <= yh + by < QUAD:
                pairs.append((2 * yh + yl, 2 * (yh + by) + turned(2 * yl, abs(by)) // 2))
    return lax.ppermute(value, ("yh", "yl"), pairs)


def split_kernel(ids_ref, key_ref, value_ref, own_ref, other_ref):
    rows = own_ref.shape[0]
    for part, out in ((ids_ref[CORE], own_ref), (1 - ids_ref[CORE], other_ref)):
        first = pl.multiple_of(part * rows, 16)
        out[:, 0:HD] = key_ref[pl.ds(first, rows), :]
        out[:, HD : 2 * HD] = value_ref[pl.ds(first, rows), :]


def table_kernel(levels_ref, ids_ref, modulation_ref, out_ref):
    feats = out_ref.shape[1]
    rows = modulation_ref[...].astype(jnp.float32)
    chosen = lax.broadcasted_iota(jnp.int32, rows.shape, 0) == levels_ref[ids_ref[SPAN]]
    row = jnp.sum(jnp.where(chosen, rows, 0.0), axis=0, keepdims=True)
    for block in range(out_ref.shape[0]):
        out_ref[block : block + 1, :] = row[:, block * feats : (block + 1) * feats]


def sums_kernel(count, has_earlier, *refs):
    out = refs[-1]
    total = jnp.zeros((1, out.shape[1]), jnp.float32)
    square = jnp.zeros((1, out.shape[1]), jnp.float32)
    for ref in refs[:count]:
        block = ref[...].astype(jnp.float32)
        total += jnp.sum(block, axis=0, keepdims=True)
        square += jnp.sum(block * block, axis=0, keepdims=True)
    if has_earlier:
        total += refs[count][0:1, :]
        square += refs[count][1:2, :]
    out[...] = jnp.zeros_like(out)
    out[0:1, :] = total
    out[1:2, :] = square


def row_sums(pieces, earlier=None):
    rest = () if earlier is None else (earlier,)
    return pl.pallas_call(
        functools.partial(sums_kernel, len(pieces), bool(rest)),
        out_shape=jax.ShapeDtypeStruct((8, pieces[0].shape[1]), jnp.float32),
        in_specs=[VMEM] * (len(pieces) + len(rest)),
        out_specs=VMEM,
        compiler_params=params(),
    )(*pieces, *rest)


def norm_kernel(ids_ref, own_ref, other_ref, table_ref, *refs):
    pieces, normed_ref = refs[:RING], refs[RING]
    feats = pieces[0].shape[0] // 2
    model_width = 4.0 * RING * feats
    stats = own_ref[...] + other_ref[...]
    mean = stats[0:1, :] / model_width
    variance = stats[1:2, :] / model_width - mean * mean
    rstd = lax.rsqrt(variance + EPSILON)
    columns = jnp.transpose(jnp.concatenate([mean, rstd, jnp.zeros((6, mean.shape[1]), jnp.float32)], axis=0))
    mean_col, rstd_col = columns[:, 0:1], columns[:, 1:2]
    blocks = table_ref.shape[0] // 2
    for slot, piece in enumerate(pieces):
        for part in range(2):
            x_at = jnp.where(part == 0, ids_ref[XH], 1 - ids_ref[XH])
            z_at = lax.rem(ids_ref[Z] + slot, RING)
            row = x_at * (2 * RING) + z_at * 2 + ids_ref[CORE]
            shift = table_ref[pl.ds(row, 1), :]
            scale = table_ref[pl.ds(blocks + row, 1), :]
            block = jnp.transpose(piece[part * feats : (part + 1) * feats, :]).astype(jnp.float32)
            block = (block - mean_col) * rstd_col * (1.0 + scale) + shift
            normed_ref[slot, part] = block.astype(jnp.bfloat16)


def project_kernel(head, ids_ref, normed_ref, *refs):
    pieces, out_ref = refs[:RING], refs[RING]
    for slot, weights in enumerate(pieces):
        y_at = lax.rem(ids_ref[Y] + slot, RING)
        half = y_at // (RING // 2)
        part = jnp.where(half == ids_ref[XH], 0, 1)
        product = None
        for side in range(2):
            xl_at = ids_ref[XL] if side == 0 else 1 - ids_ref[XL]
            z_at = 2 * (y_at - half * (RING // 2)) + xl_at
            place = lax.rem(z_at + RING - ids_ref[Z], RING)
            term = jnp.dot(normed_ref[place, part], weights[2 * side + head], preferred_element_type=jnp.float32)
            product = term if product is None else product + term
        if slot == 0:
            out_ref[...] = product
        else:
            out_ref[...] += product


def project(head, ids, normed, pieces):
    return pl.pallas_call(
        functools.partial(project_kernel, head),
        out_shape=jax.ShapeDtypeStruct((normed.shape[2], 2 * HD), jnp.float32),
        in_specs=[SMEM] + [VMEM] * (1 + RING),
        out_specs=VMEM,
        compiler_params=params(),
    )(ids, normed, *pieces)


def join_kernel(mine_ref, theirs_ref, out_ref):
    rows = mine_ref.shape[0]
    total = (mine_ref[...] + theirs_ref[...]).astype(jnp.bfloat16)
    out_ref[0:rows, :] = total[:, 0:HD]
    for b in range(rows // HD):
        out_ref[rows + b * HD : rows + (b + 1) * HD, :] = jnp.transpose(
            total[b * HD : (b + 1) * HD, HD : 2 * HD]
        )


def scan_keys(later, flips, ids_ref, visible_ref, counts_ref, q_t, kv_refs, stat, acc):
    factor = LOG2E * HD ** (-0.5)
    quad, place = ids_ref[YH], ids_ref[PLACE]
    q_span = jnp.minimum((quad + later) * QUAD + turned(place, later), QUAD * QUAD - 1)
    for flip, kv_ref in zip(flips, kv_refs):
        k_span = quad * QUAD + (place ^ flip)
        span_len = kv_ref.shape[0] // 2
        seen = visible_ref[q_span, k_span] == 1
        if later == 0:
            seen = (k_span == q_span) if flip == 0 else jnp.logical_and(seen, k_span < q_span)
        else:
            seen = jnp.logical_and(seen, quad + later < QUAD)

        @pl.when(seen)
        def _():
            scores = jnp.dot(kv_ref[0:span_len, :], q_t[...], preferred_element_type=jnp.float32)
            live = lax.broadcasted_iota(jnp.int32, scores.shape, 0) < counts_ref[k_span]
            scores = jnp.where(live, scores * factor, NEG_BIG)
            best = stat[0:1, :]
            top = jnp.maximum(best, jnp.max(scores, axis=0, keepdims=True))
            weights = jnp.exp2(scores - top)
            fading = jnp.exp2(best - top)
            stat[8:9, :] = stat[8:9, :] * fading + jnp.sum(weights, axis=0, keepdims=True)
            stat[0:1, :] = top
            values = jnp.concatenate(
                [kv_ref[span_len + b * HD : span_len + (b + 1) * HD, :] for b in range(span_len // HD)], axis=1
            )
            acc[...] = acc[...] * fading + jnp.dot(
                values, weights.astype(jnp.bfloat16), preferred_element_type=jnp.float32
            )


def begin_kernel(ids_ref, visible_ref, counts_ref, q0, q1, q2, q3, kv_ref, q_t, stat, acc):
    for later, q_ref in enumerate((q0, q1, q2, q3)):
        q_t[later] = jnp.transpose(q_ref[...])
        stat[later, 0:8, :] = jnp.full((8, stat.shape[2]), NEG_BIG, jnp.float32)
        stat[later, 8:16, :] = jnp.zeros((8, stat.shape[2]), jnp.float32)
        acc[later] = jnp.zeros(acc.shape[1:], jnp.float32)
        scan_keys(
            later, (0,), ids_ref, visible_ref, counts_ref, q_t.at[later], (kv_ref,), stat.at[later], acc.at[later]
        )


def middle_kernel(ids_ref, visible_ref, counts_ref, q_t, stat_in, acc_in, kv_ref, stat, acc):
    for later in range(QUAD):
        scan_keys(
            later, (2,), ids_ref, visible_ref, counts_ref, q_t.at[later], (kv_ref,), stat.at[later], acc.at[later]
        )


def finish_kernel(later, ids_ref, visible_ref, counts_ref, q_t, stat_in, acc_in, kv1, kv3, out_ref, stat, acc):
    span_len = out_ref.shape[0] - STAT_ROWS

    @pl.when(ids_ref[YH] + later < QUAD)
    def _():
        stat[...] = stat_in[later]
        acc[...] = acc_in[later]
        scan_keys(later, (1, 3), ids_ref, visible_ref, counts_ref, q_t.at[later], (kv1, kv3), stat, acc)
        best = stat[0:1, :]
        high = best.astype(jnp.bfloat16).astype(jnp.float32)
        low = (best - high).astype(jnp.bfloat16).astype(jnp.float32)
        scale = jnp.where(best > 0.5 * NEG_BIG, jnp.exp2((best - high) - low), 0.0)
        total = stat[8:9, :] * scale
        total_high = total.astype(jnp.bfloat16).astype(jnp.float32)
        stats = jnp.concatenate([high, low, total_high, total - total_high], axis=0)
        result = (acc[...] * scale).astype(jnp.bfloat16)
        for b in range(span_len // HD):
            out_ref[b * HD : (b + 1) * HD, :] = result[:, b * HD : (b + 1) * HD]
        stats = jnp.concatenate([stats[:, b * HD : (b + 1) * HD] for b in range(span_len // HD)], axis=0)
        out_ref[span_len:, :] = stats.astype(jnp.bfloat16)

    @pl.when(ids_ref[YH] + later >= QUAD)
    def _():
        out_ref[...] = jnp.zeros_like(out_ref)


def merge_kernel(ids_ref, counts_ref, part0, part1, part2, part3, out_ref):
    span_len = out_ref.shape[0]
    parts = (part0, part1, part2, part3)
    blocks = span_len // HD
    for block in range(blocks):
        bests, totals = [], []
        for earlier, part in enumerate(parts):
            stat = part[span_len:, :].astype(jnp.float32)[block * 4 : (block + 1) * 4, :]
            sent = ids_ref[YH] >= earlier
            bests.append(jnp.where(sent, stat[0:1] + stat[1:2], NEG_BIG))
            totals.append(jnp.where(sent, stat[2:3] + stat[3:4], 0.0))
        top = functools.reduce(jnp.maximum, bests)
        share = [jnp.exp2(b - top) for b in bests]
        total = sum(s * t for s, t in zip(share, totals))
        rows = slice(block * HD, (block + 1) * HD)
        result = sum(s * part[rows, :].astype(jnp.float32) for s, part in zip(share, parts))
        slot = lax.broadcasted_iota(jnp.int32, total.shape, 1) + block * HD
        result = jnp.where(slot < counts_ref[ids_ref[SPAN]], result / total, 0.0)
        out_ref[rows, :] = jnp.transpose(result).astype(jnp.bfloat16)


def on_device(tokens, queries, key_weight, value_weight, modulation, levels, visible, counts):
    span_id = lax.axis_index(SPAN_AXES)
    ids = jnp.stack(
        [
            span_id,
            lax.axis_index("yh"),
            lax.axis_index(("yl", "xl")),
            lax.axis_index(("yh", "yl")),
            lax.axis_index("xl"),
            lax.axis_index("xh"),
            lax.axis_index("z"),
            lax.axis_index("c"),
        ]
    ).astype(jnp.int32)
    span_len, feats = tokens.shape
    depth = key_weight.shape[0] // 2

    w_type = jax.ShapeDtypeStruct((depth, 2 * HD), jnp.bfloat16)
    w_own, w_other = pl.pallas_call(
        split_kernel,
        out_shape=(w_type, w_type),
        in_specs=[SMEM, VMEM, VMEM],
        out_specs=(VMEM, VMEM),
        compiler_params=params(),
    )(ids, key_weight, value_weight)
    w_chip = jnp.stack([w_own, shifted(w_other, "c", 2, 1)])
    w0 = jnp.concatenate([w_chip, shifted(w_chip, "xl", 2, 1)], axis=0)

    a0 = jnp.transpose(tokens)
    x0 = jnp.concatenate([a0, shifted(a0, "xh", 2, 1)], axis=0)

    q1, q2, q3 = (moved(queries, -later) for later in (1, 2, 3))
    w0, q1, q3 = lax.optimization_barrier((w0, q1, q3))

    x_up, x_down, w_up, w_down = [x0], [x0], [w0], [w0]
    y_axes = ("yh", "yl")
    for step in range(4):
        x_up.append(shifted(x_up[-1], "z", RING, 1))
        if step < 3:
            w_up.append(shifted(w_up[-1], y_axes, RING, 1))
            x_down.append(shifted(x_down[-1], "z", RING, -1))
        w_down.append(shifted(w_down[-1], y_axes, RING, -1))
    x_slots = [x0, x_down[1], x_down[2], x_down[3], x_up[4], x_up[3], x_up[2], x_up[1]]
    w_slots = [w0, w_down[1], w_down[2], w_down[3], w_down[4], w_up[3], w_up[2], w_up[1]]

    early = row_sums(x_slots[:4] + x_slots[5:])
    own_sums = row_sums([x_slots[4]], early)
    other_sums = shifted(own_sums, "c", 2, 1)
    table = pl.pallas_call(
        table_kernel,
        out_shape=jax.ShapeDtypeStruct((modulation.shape[1] // feats, feats), jnp.float32),
        in_specs=[SMEM, SMEM, VMEM],
        out_specs=VMEM,
        compiler_params=params(),
    )(levels, ids, modulation)
    normed = pl.pallas_call(
        norm_kernel,
        out_shape=jax.ShapeDtypeStruct((RING, 2, span_len, feats), jnp.bfloat16),
        in_specs=[SMEM] + [VMEM] * (3 + RING),
        out_specs=VMEM,
        compiler_params=params(),
    )(ids, own_sums, other_sums, table, *x_slots)
    normed, q2 = lax.optimization_barrier((normed, q2))
    theirs = shifted(project(1, ids, normed, w_slots), "c", 2, 1)
    mine = project(0, ids, normed, w_slots)
    kv0 = pl.pallas_call(
        join_kernel,
        out_shape=jax.ShapeDtypeStruct((2 * span_len, HD), jnp.bfloat16),
        in_specs=[VMEM, VMEM],
        out_specs=VMEM,
        compiler_params=params(),
    )(mine, theirs)

    kv1 = shifted(kv0, "xl", 2, 1)
    kv2 = shifted(kv0, "yl", 2, 1)
    kv3 = lax.ppermute(kv0, ("yl", "xl"), [(i, 3 - i) for i in range(4)])
    scalars = (ids, visible, counts)
    q_type = jax.ShapeDtypeStruct((QUAD, HD, span_len), jnp.bfloat16)
    stat_type = jax.ShapeDtypeStruct((QUAD, 16, span_len), jnp.float32)
    acc_type = jax.ShapeDtypeStruct((QUAD, HD, span_len), jnp.float32)
    q_t, stat, acc = pl.pallas_call(
        begin_kernel,
        out_shape=(q_type, stat_type, acc_type),
        in_specs=[SMEM] * 3 + [VMEM] * 5,
        out_specs=(VMEM,) * 3,
        compiler_params=params(),
    )(*scalars, queries, q1, q2, q3, kv0)
    stat, acc = pl.pallas_call(
        middle_kernel,
        out_shape=(stat_type, acc_type),
        in_specs=[SMEM] * 3 + [VMEM] * 4,
        out_specs=(VMEM,) * 2,
        input_output_aliases={4: 0, 5: 1},
        compiler_params=params(),
    )(*scalars, q_t, stat, acc, kv2)
    parts = [None] * QUAD
    for later in (2, 3, 1, 0):
        part = pl.pallas_call(
            functools.partial(finish_kernel, later),
            out_shape=jax.ShapeDtypeStruct((span_len + STAT_ROWS, HD), jnp.bfloat16),
            in_specs=[SMEM] * 3 + [VMEM] * 5,
            out_specs=VMEM,
            scratch_shapes=[pltpu.VMEM((16, span_len), jnp.float32), pltpu.VMEM((HD, span_len), jnp.float32)],
            compiler_params=params(),
        )(*scalars, q_t, stat, acc, kv1, kv3)
        parts[later] = moved(part, later) if later else part
    return pl.pallas_call(
        merge_kernel,
        out_shape=jax.ShapeDtypeStruct((span_len, HD), jnp.bfloat16),
        in_specs=[SMEM, SMEM] + [VMEM] * QUAD,
        out_specs=VMEM,
        compiler_params=params(),
    )(ids, counts, *parts)


def solution(mesh):
    fine = Mesh(mesh.devices.reshape(SIZES), SPAN_AXES + FSDP_AXES)
    spread = P(SPAN_AXES, FSDP_AXES)
    return jax.shard_map(
        on_device,
        mesh=fine,
        in_specs=(spread, spread, spread, spread, P(), P(), P(), P()),
        out_specs=spread,
        check_vma=False,
    )
```

```python
import functools

import jax
import jax.numpy as jnp
from jax import lax
from jax.experimental import pallas as pl
from jax.experimental.pallas import tpu as pltpu
from jax.sharding import Mesh, PartitionSpec as P

HD = 128
EPSILON = 1e-06
NEG_BIG = -1e30
LOG2E = 1.4426950408889634
SPAN_AXES = ("yh", "yl", "xl")
FSDP_AXES = ("xh", "z", "c")
SIZES = (4, 2, 2, 2, 8, 2)
QUAD = 4
RING = 8
STAT_ROWS = 16
SPAN, YH, PLACE, Y, XL, XH, Z, CORE, LEVEL = range(9)

VMEM = pl.BlockSpec(memory_space=pltpu.VMEM)
SMEM = pl.BlockSpec(memory_space=pltpu.SMEM)


def params(mib=12):
    return pltpu.CompilerParams(vmem_limit_bytes=mib * 1024 * 1024)


def shifted(value, axis, size, by):
    return lax.ppermute(value, axis, [(i, (i + by) % size) for i in range(size)])


def turned(place, later):
    return place ^ 2 if later == 2 else place


def moved(value, by):
    pairs = []
    for yh in range(QUAD):
        for yl in range(2):
            if 0 <= yh + by < QUAD:
                pairs.append((2 * yh + yl, 2 * (yh + by) + turned(2 * yl, abs(by)) // 2))
    return lax.ppermute(value, ("yh", "yl"), pairs)


def stack_kernel(*refs):
    out_ref, first = refs[-1], 0
    for ref in refs[:-1]:
        out_ref[first : first + ref.shape[0]] = ref[...]
        first += ref.shape[0]


def stacked(*pieces):
    rows = sum(piece.shape[0] for piece in pieces)
    return pl.pallas_call(
        stack_kernel,
        out_shape=jax.ShapeDtypeStruct((rows,) + pieces[0].shape[1:], pieces[0].dtype),
        in_specs=[VMEM] * len(pieces),
        out_specs=VMEM,
        compiler_params=params(),
    )(*pieces)


def split_kernel(ids_ref, key_ref, value_ref, own_ref, other_ref):
    rows = own_ref.shape[0]
    for part, out in ((ids_ref[CORE], own_ref), (1 - ids_ref[CORE], other_ref)):
        first = pl.multiple_of(part * rows, 16)
        out[:, 0:HD] = key_ref[pl.ds(first, rows), :]
        out[:, HD : 2 * HD] = value_ref[pl.ds(first, rows), :]


def table_kernel(levels_ref, ids_ref, modulation_ref, out_ref):
    feats = out_ref.shape[1]
    rows = modulation_ref[...].astype(jnp.float32)
    chosen = lax.broadcasted_iota(jnp.int32, rows.shape, 0) == levels_ref[ids_ref[SPAN]]
    row = jnp.sum(jnp.where(chosen, rows, 0.0), axis=0, keepdims=True)
    for block in range(out_ref.shape[0]):
        out_ref[block : block + 1, :] = row[:, block * feats : (block + 1) * feats]


def sums_kernel(count, has_earlier, *refs):
    out = refs[-1]
    total = jnp.zeros((1, out.shape[1]), jnp.float32)
    square = jnp.zeros((1, out.shape[1]), jnp.float32)
    for ref in refs[:count]:
        block = ref[...].astype(jnp.float32)
        total += jnp.sum(block, axis=0, keepdims=True)
        square += jnp.sum(block * block, axis=0, keepdims=True)
    if has_earlier:
        total += refs[count][0:1, :]
        square += refs[count][1:2, :]
    out[...] = jnp.zeros_like(out)
    out[0:1, :] = total
    out[1:2, :] = square


def row_sums(pieces, earlier=None):
    rest = () if earlier is None else (earlier,)
    return pl.pallas_call(
        functools.partial(sums_kernel, len(pieces), bool(rest)),
        out_shape=jax.ShapeDtypeStruct((8, pieces[0].shape[1]), jnp.float32),
        in_specs=[VMEM] * (len(pieces) + len(rest)),
        out_specs=VMEM,
        compiler_params=params(),
    )(*pieces, *rest)


def norm_kernel(ids_ref, own_ref, other_ref, table_ref, *refs):
    pieces, normed_ref = refs[:RING], refs[RING]
    feats = pieces[0].shape[0] // 2
    model_width = 4.0 * RING * feats
    stats = own_ref[...] + other_ref[...]
    mean = stats[0:1, :] / model_width
    variance = stats[1:2, :] / model_width - mean * mean
    rstd = lax.rsqrt(variance + EPSILON)
    columns = jnp.transpose(jnp.concatenate([mean, rstd, jnp.zeros((6, mean.shape[1]), jnp.float32)], axis=0))
    mean_col, rstd_col = columns[:, 0:1], columns[:, 1:2]
    blocks = table_ref.shape[0] // 2
    for slot, piece in enumerate(pieces):
        for part in range(2):
            x_at = jnp.where(part == 0, ids_ref[XH], 1 - ids_ref[XH])
            z_at = lax.rem(ids_ref[Z] + slot, RING)
            row = x_at * (2 * RING) + z_at * 2 + ids_ref[CORE]
            shift = table_ref[pl.ds(row, 1), :]
            scale = table_ref[pl.ds(blocks + row, 1), :]
            block = jnp.transpose(piece[part * feats : (part + 1) * feats, :]).astype(jnp.float32)
            block = (block - mean_col) * rstd_col * (1.0 + scale) + shift
            normed_ref[slot, part] = block.astype(jnp.bfloat16)


def project_kernel(head, ids_ref, normed_ref, *refs):
    pieces, out_ref = refs[:RING], refs[RING]
    for slot, weights in enumerate(pieces):
        y_at = lax.rem(ids_ref[Y] + slot, RING)
        half = y_at // (RING // 2)
        part = jnp.where(half == ids_ref[XH], 0, 1)
        product = None
        for side in range(2):
            xl_at = ids_ref[XL] if side == 0 else 1 - ids_ref[XL]
            z_at = 2 * (y_at - half * (RING // 2)) + xl_at
            place = lax.rem(z_at + RING - ids_ref[Z], RING)
            term = jnp.dot(normed_ref[place, part], weights[2 * side + head], preferred_element_type=jnp.float32)
            product = term if product is None else product + term
        if slot == 0:
            out_ref[...] = product
        else:
            out_ref[...] += product


def project(head, ids, normed, pieces):
    return pl.pallas_call(
        functools.partial(project_kernel, head),
        out_shape=jax.ShapeDtypeStruct((normed.shape[2], 2 * HD), jnp.float32),
        in_specs=[SMEM] + [VMEM] * (1 + RING),
        out_specs=VMEM,
        compiler_params=params(),
    )(ids, normed, *pieces)


def join_kernel(mine_ref, theirs_ref, out_ref):
    rows = mine_ref.shape[0]
    total = (mine_ref[...] + theirs_ref[...]).astype(jnp.bfloat16)
    out_ref[0:rows, :] = total[:, 0:HD]
    for b in range(rows // HD):
        out_ref[rows + b * HD : rows + (b + 1) * HD, :] = jnp.transpose(
            total[b * HD : (b + 1) * HD, HD : 2 * HD]
        )


def scan_keys(later, flips, ids_ref, visible_ref, counts_ref, q_t, kv_refs, stat, acc):
    factor = LOG2E * HD ** (-0.5)
    quad, place = ids_ref[YH], ids_ref[PLACE]
    q_span = jnp.minimum((quad + later) * QUAD + turned(place, later), QUAD * QUAD - 1)
    for flip, kv_ref in zip(flips, kv_refs):
        k_span = quad * QUAD + (place ^ flip)
        span_len = kv_ref.shape[0] // 2
        seen = visible_ref[q_span, k_span] == 1
        if later == 0:
            seen = (k_span == q_span) if flip == 0 else jnp.logical_and(seen, k_span < q_span)
        else:
            seen = jnp.logical_and(seen, quad + later < QUAD)

        @pl.when(seen)
        def _():
            scores = jnp.dot(kv_ref[0:span_len, :], q_t[...], preferred_element_type=jnp.float32)
            live = lax.broadcasted_iota(jnp.int32, scores.shape, 0) < counts_ref[k_span]
            scores = jnp.where(live, scores * factor, NEG_BIG)
            best = stat[0:1, :]
            top = jnp.maximum(best, jnp.max(scores, axis=0, keepdims=True))
            weights = jnp.exp2(scores - top)
            fading = jnp.exp2(best - top)
            stat[8:9, :] = stat[8:9, :] * fading + jnp.sum(weights, axis=0, keepdims=True)
            stat[0:1, :] = top
            values = jnp.concatenate(
                [kv_ref[span_len + b * HD : span_len + (b + 1) * HD, :] for b in range(span_len // HD)], axis=1
            )
            acc[...] = acc[...] * fading + jnp.dot(
                values, weights.astype(jnp.bfloat16), preferred_element_type=jnp.float32
            )


def begin_kernel(ids_ref, visible_ref, counts_ref, q0, q1, q2, q3, kv_ref, q_t, stat, acc):
    for later, q_ref in enumerate((q0, q1, q2, q3)):
        q_t[later] = jnp.transpose(q_ref[...])
        stat[later, 0:8, :] = jnp.full((8, stat.shape[2]), NEG_BIG, jnp.float32)
        stat[later, 8:16, :] = jnp.zeros((8, stat.shape[2]), jnp.float32)
        acc[later] = jnp.zeros(acc.shape[1:], jnp.float32)
        scan_keys(
            later, (0,), ids_ref, visible_ref, counts_ref, q_t.at[later], (kv_ref,), stat.at[later], acc.at[later]
        )


def middle_kernel(ids_ref, visible_ref, counts_ref, q_t, stat_in, acc_in, kv_ref, stat, acc):
    for later in range(QUAD):
        scan_keys(
            later, (2,), ids_ref, visible_ref, counts_ref, q_t.at[later], (kv_ref,), stat.at[later], acc.at[later]
        )


def finish_kernel(later, ids_ref, visible_ref, counts_ref, q_t, stat_in, acc_in, kv1, kv3, out_ref, stat, acc):
    span_len = out_ref.shape[0] - STAT_ROWS

    @pl.when(ids_ref[YH] + later < QUAD)
    def _():
        stat[...] = stat_in[later]
        acc[...] = acc_in[later]
        scan_keys(later, (1, 3), ids_ref, visible_ref, counts_ref, q_t.at[later], (kv1, kv3), stat, acc)
        best = stat[0:1, :]
        high = best.astype(jnp.bfloat16).astype(jnp.float32)
        low = (best - high).astype(jnp.bfloat16).astype(jnp.float32)
        scale = jnp.where(best > 0.5 * NEG_BIG, jnp.exp2((best - high) - low), 0.0)
        total = stat[8:9, :] * scale
        total_high = total.astype(jnp.bfloat16).astype(jnp.float32)
        stats = jnp.concatenate([high, low, total_high, total - total_high], axis=0)
        result = (acc[...] * scale).astype(jnp.bfloat16)
        for b in range(span_len // HD):
            out_ref[b * HD : (b + 1) * HD, :] = result[:, b * HD : (b + 1) * HD]
        stats = jnp.concatenate([stats[:, b * HD : (b + 1) * HD] for b in range(span_len // HD)], axis=0)
        out_ref[span_len:, :] = stats.astype(jnp.bfloat16)

    @pl.when(ids_ref[YH] + later >= QUAD)
    def _():
        out_ref[...] = jnp.zeros_like(out_ref)


def merge_kernel(ids_ref, counts_ref, part0, part1, part2, part3, out_ref):
    span_len = out_ref.shape[0]
    parts = (part0, part1, part2, part3)
    blocks = span_len // HD
    for block in range(blocks):
        bests, totals = [], []
        for earlier, part in enumerate(parts):
            stat = part[span_len:, :].astype(jnp.float32)[block * 4 : (block + 1) * 4, :]
            sent = ids_ref[YH] >= earlier
            bests.append(jnp.where(sent, stat[0:1] + stat[1:2], NEG_BIG))
            totals.append(jnp.where(sent, stat[2:3] + stat[3:4], 0.0))
        top = functools.reduce(jnp.maximum, bests)
        share = [jnp.exp2(b - top) for b in bests]
        total = sum(s * t for s, t in zip(share, totals))
        rows = slice(block * HD, (block + 1) * HD)
        result = sum(s * part[rows, :].astype(jnp.float32) for s, part in zip(share, parts))
        slot = lax.broadcasted_iota(jnp.int32, total.shape, 1) + block * HD
        result = jnp.where(slot < counts_ref[ids_ref[SPAN]], result / total, 0.0)
        out_ref[rows, :] = jnp.transpose(result).astype(jnp.bfloat16)


def on_device(tokens, queries, key_weight, value_weight, modulation, levels, visible, counts):
    span_id = lax.axis_index(SPAN_AXES)
    ids = jnp.stack(
        [
            span_id,
            lax.axis_index("yh"),
            lax.axis_index(("yl", "xl")),
            lax.axis_index(("yh", "yl")),
            lax.axis_index("xl"),
            lax.axis_index("xh"),
            lax.axis_index("z"),
            lax.axis_index("c"),
        ]
    ).astype(jnp.int32)
    span_len, feats = tokens.shape
    depth = key_weight.shape[0] // 2

    def rows_of(part):
        first = part * depth
        return jnp.concatenate(
            [lax.dynamic_slice_in_dim(w, first, depth, 0) for w in (key_weight, value_weight)], axis=1
        )

    core = lax.axis_index("c")
    w_own, w_other = rows_of(core), rows_of(1 - core)
    w_other, ids = lax.optimization_barrier((w_other, ids))
    w_chip = jnp.stack([w_own, shifted(w_other, "c", 2, 1)])
    w0 = stacked(w_chip, shifted(w_chip, "xl", 2, 1))

    a0 = jnp.transpose(tokens)
    x0 = stacked(a0, shifted(a0, "xh", 2, 1))

    q1, q2, q3 = (moved(queries, -later) for later in (1, 2, 3))
    w0, q1, q3 = lax.optimization_barrier((w0, q1, q3))

    x_up, x_down, w_up, w_down = [x0], [x0], [w0], [w0]
    y_axes = ("yh", "yl")
    for step in range(4):
        x_up.append(shifted(x_up[-1], "z", RING, 1))
        if step < 3:
            w_up.append(shifted(w_up[-1], y_axes, RING, 1))
            x_down.append(shifted(x_down[-1], "z", RING, -1))
        w_down.append(shifted(w_down[-1], y_axes, RING, -1))
    x_slots = [x0, x_down[1], x_down[2], x_down[3], x_up[4], x_up[3], x_up[2], x_up[1]]
    w_slots = [w0, w_down[1], w_down[2], w_down[3], w_down[4], w_up[3], w_up[2], w_up[1]]

    early = row_sums(x_slots[:4] + x_slots[5:])
    own_sums = row_sums([x_slots[4]], early)
    other_sums = shifted(own_sums, "c", 2, 1)
    table = pl.pallas_call(
        table_kernel,
        out_shape=jax.ShapeDtypeStruct((modulation.shape[1] // feats, feats), jnp.float32),
        in_specs=[SMEM, SMEM, VMEM],
        out_specs=VMEM,
        compiler_params=params(),
    )(levels, ids, modulation)
    normed = pl.pallas_call(
        norm_kernel,
        out_shape=jax.ShapeDtypeStruct((RING, 2, span_len, feats), jnp.bfloat16),
        in_specs=[SMEM] + [VMEM] * (3 + RING),
        out_specs=VMEM,
        compiler_params=params(),
    )(ids, own_sums, other_sums, table, *x_slots)
    normed, q2 = lax.optimization_barrier((normed, q2))
    theirs = shifted(project(1, ids, normed, w_slots), "c", 2, 1)
    mine = project(0, ids, normed, w_slots)
    kv0 = pl.pallas_call(
        join_kernel,
        out_shape=jax.ShapeDtypeStruct((2 * span_len, HD), jnp.bfloat16),
        in_specs=[VMEM, VMEM],
        out_specs=VMEM,
        compiler_params=params(),
    )(mine, theirs)

    kv1 = shifted(kv0, "xl", 2, 1)
    kv2 = shifted(kv0, "yl", 2, 1)
    kv3 = lax.ppermute(kv0, ("yl", "xl"), [(i, 3 - i) for i in range(4)])
    scalars = (ids, visible, counts)
    q_type = jax.ShapeDtypeStruct((QUAD, HD, span_len), jnp.bfloat16)
    stat_type = jax.ShapeDtypeStruct((QUAD, 16, span_len), jnp.float32)
    acc_type = jax.ShapeDtypeStruct((QUAD, HD, span_len), jnp.float32)
    q_t, stat, acc = pl.pallas_call(
        begin_kernel,
        out_shape=(q_type, stat_type, acc_type),
        in_specs=[SMEM] * 3 + [VMEM] * 5,
        out_specs=(VMEM,) * 3,
        compiler_params=params(),
    )(*scalars, queries, q1, q2, q3, kv0)
    stat, acc = pl.pallas_call(
        middle_kernel,
        out_shape=(stat_type, acc_type),
        in_specs=[SMEM] * 3 + [VMEM] * 4,
        out_specs=(VMEM,) * 2,
        input_output_aliases={4: 0, 5: 1},
        compiler_params=params(),
    )(*scalars, q_t, stat, acc, kv2)
    parts = [None] * QUAD
    for later in (2, 3, 1, 0):
        part = pl.pallas_call(
            functools.partial(finish_kernel, later),
            out_shape=jax.ShapeDtypeStruct((span_len + STAT_ROWS, HD), jnp.bfloat16),
            in_specs=[SMEM] * 3 + [VMEM] * 5,
            out_specs=VMEM,
            scratch_shapes=[pltpu.VMEM((16, span_len), jnp.float32), pltpu.VMEM((HD, span_len), jnp.float32)],
            compiler_params=params(),
        )(*scalars, q_t, stat, acc, kv1, kv3)
        parts[later] = moved(part, later) if later else part
    return pl.pallas_call(
        merge_kernel,
        out_shape=jax.ShapeDtypeStruct((span_len, HD), jnp.bfloat16),
        in_specs=[SMEM, SMEM] + [VMEM] * QUAD,
        out_specs=VMEM,
        compiler_params=params(),
    )(ids, counts, *parts)


def solution(mesh):
    fine = Mesh(mesh.devices.reshape(SIZES), SPAN_AXES + FSDP_AXES)
    spread = P(SPAN_AXES, FSDP_AXES)
    return jax.shard_map(
        on_device,
        mesh=fine,
        in_specs=(spread, spread, spread, spread, P(), P(), P(), P()),
        out_specs=spread,
        check_vma=False,
    )
```

```python
import functools

import jax
import jax.numpy as jnp
from jax import lax
from jax.experimental import pallas as pl
from jax.experimental.pallas import tpu as pltpu
from jax.sharding import Mesh, PartitionSpec as P

HD = 128
EPSILON = 1e-06
NEG_BIG = -1e30
LOG2E = 1.4426950408889634
SPAN_AXES = ("yh", "yl", "xl")
FSDP_AXES = ("xh", "z", "c")
SIZES = (4, 2, 2, 2, 8, 2)
QUAD = 4
RING = 8
STAT_ROWS = 16
SPAN, YH, PLACE, Y, XL, XH, Z, CORE, LEVEL = range(9)

VMEM = pl.BlockSpec(memory_space=pltpu.VMEM)
SMEM = pl.BlockSpec(memory_space=pltpu.SMEM)


def params(mib=12):
    return pltpu.CompilerParams(vmem_limit_bytes=mib * 1024 * 1024)


def shifted(value, axis, size, by):
    return lax.ppermute(value, axis, [(i, (i + by) % size) for i in range(size)])


def turned(place, later):
    return place ^ 2 if later == 2 else place


def moved(value, by):
    pairs = []
    for yh in range(QUAD):
        for yl in range(2):
            if 0 <= yh + by < QUAD:
                pairs.append((2 * yh + yl, 2 * (yh + by) + turned(2 * yl, abs(by)) // 2))
    return lax.ppermute(value, ("yh", "yl"), pairs)


def stack_kernel(*refs):
    out_ref, first = refs[-1], 0
    for ref in refs[:-1]:
        out_ref[first : first + ref.shape[0]] = ref[...]
        first += ref.shape[0]


def stacked(*pieces):
    rows = sum(piece.shape[0] for piece in pieces)
    return pl.pallas_call(
        stack_kernel,
        out_shape=jax.ShapeDtypeStruct((rows,) + pieces[0].shape[1:], pieces[0].dtype),
        in_specs=[VMEM] * len(pieces),
        out_specs=VMEM,
        compiler_params=params(),
    )(*pieces)


def split_kernel(ids_ref, key_ref, value_ref, own_ref, other_ref):
    rows = own_ref.shape[0]
    for part, out in ((ids_ref[CORE], own_ref), (1 - ids_ref[CORE], other_ref)):
        first = pl.multiple_of(part * rows, 16)
        out[:, 0:HD] = key_ref[pl.ds(first, rows), :]
        out[:, HD : 2 * HD] = value_ref[pl.ds(first, rows), :]


def table_kernel(levels_ref, ids_ref, modulation_ref, out_ref):
    feats = out_ref.shape[1]
    rows = modulation_ref[...].astype(jnp.float32)
    chosen = lax.broadcasted_iota(jnp.int32, rows.shape, 0) == levels_ref[ids_ref[SPAN]]
    row = jnp.sum(jnp.where(chosen, rows, 0.0), axis=0, keepdims=True)
    for block in range(out_ref.shape[0]):
        out_ref[block : block + 1, :] = row[:, block * feats : (block + 1) * feats]


def sums_kernel(count, has_earlier, *refs):
    out = refs[-1]
    total = jnp.zeros((1, out.shape[1]), jnp.float32)
    square = jnp.zeros((1, out.shape[1]), jnp.float32)
    for ref in refs[:count]:
        block = ref[...].astype(jnp.float32)
        total += jnp.sum(block, axis=0, keepdims=True)
        square += jnp.sum(block * block, axis=0, keepdims=True)
    if has_earlier:
        total += refs[count][0:1, :]
        square += refs[count][1:2, :]
    out[...] = jnp.zeros_like(out)
    out[0:1, :] = total
    out[1:2, :] = square


def row_sums(pieces, earlier=None):
    rest = () if earlier is None else (earlier,)
    return pl.pallas_call(
        functools.partial(sums_kernel, len(pieces), bool(rest)),
        out_shape=jax.ShapeDtypeStruct((8, pieces[0].shape[1]), jnp.float32),
        in_specs=[VMEM] * (len(pieces) + len(rest)),
        out_specs=VMEM,
        compiler_params=params(),
    )(*pieces, *rest)


def norm_kernel(ids_ref, own_ref, other_ref, table_ref, *refs):
    pieces, normed_ref = refs[:RING], refs[RING]
    feats = pieces[0].shape[0] // 2
    model_width = 4.0 * RING * feats
    stats = own_ref[...] + other_ref[...]
    mean = stats[0:1, :] / model_width
    variance = stats[1:2, :] / model_width - mean * mean
    rstd = lax.rsqrt(variance + EPSILON)
    columns = jnp.transpose(jnp.concatenate([mean, rstd, jnp.zeros((6, mean.shape[1]), jnp.float32)], axis=0))
    mean_col, rstd_col = columns[:, 0:1], columns[:, 1:2]
    blocks = table_ref.shape[0] // 2
    for slot, piece in enumerate(pieces):
        for part in range(2):
            x_at = jnp.where(part == 0, ids_ref[XH], 1 - ids_ref[XH])
            z_at = lax.rem(ids_ref[Z] + slot, RING)
            row = x_at * (2 * RING) + z_at * 2 + ids_ref[CORE]
            shift = table_ref[pl.ds(row, 1), :]
            scale = table_ref[pl.ds(blocks + row, 1), :]
            block = jnp.transpose(piece[part * feats : (part + 1) * feats, :]).astype(jnp.float32)
            block = (block - mean_col) * rstd_col * (1.0 + scale) + shift
            normed_ref[slot, part] = block.astype(jnp.bfloat16)


def project_kernel(head, slots, has_earlier, ids_ref, normed_ref, *refs):
    pieces, out_ref = refs[: len(slots)], refs[-1]
    for k, (slot, weights) in enumerate(zip(slots, pieces)):
        y_at = lax.rem(ids_ref[Y] + slot, RING)
        half = y_at // (RING // 2)
        part = jnp.where(half == ids_ref[XH], 0, 1)
        product = None
        for side in range(2):
            xl_at = ids_ref[XL] if side == 0 else 1 - ids_ref[XL]
            z_at = 2 * (y_at - half * (RING // 2)) + xl_at
            place = lax.rem(z_at + RING - ids_ref[Z], RING)
            term = jnp.dot(normed_ref[place, part], weights[2 * side + head], preferred_element_type=jnp.float32)
            product = term if product is None else product + term
        if k == 0:
            out_ref[...] = refs[len(slots)][...] + product if has_earlier else product
        else:
            out_ref[...] += product


def project(head, slots, ids, normed, pieces, earlier=()):
    return pl.pallas_call(
        functools.partial(project_kernel, head, slots, bool(earlier)),
        out_shape=jax.ShapeDtypeStruct((normed.shape[2], 2 * HD), jnp.float32),
        in_specs=[SMEM] + [VMEM] * (1 + len(pieces) + len(earlier)),
        out_specs=VMEM,
        compiler_params=params(),
    )(ids, normed, *pieces, *earlier)


def join_kernel(mine_ref, theirs_ref, out_ref):
    rows = mine_ref.shape[0]
    total = (mine_ref[...] + theirs_ref[...]).astype(jnp.bfloat16)
    out_ref[0:rows, :] = total[:, 0:HD]
    for b in range(rows // HD):
        out_ref[rows + b * HD : rows + (b + 1) * HD, :] = jnp.transpose(
            total[b * HD : (b + 1) * HD, HD : 2 * HD]
        )


def scan_keys(later, flips, ids_ref, visible_ref, counts_ref, q_t, kv_refs, stat, acc):
    factor = LOG2E * HD ** (-0.5)
    quad, place = ids_ref[YH], ids_ref[PLACE]
    q_span = jnp.minimum((quad + later) * QUAD + turned(place, later), QUAD * QUAD - 1)
    for flip, kv_ref in zip(flips, kv_refs):
        k_span = quad * QUAD + (place ^ flip)
        span_len = kv_ref.shape[0] // 2
        seen = visible_ref[q_span, k_span] == 1
        if later == 0:
            seen = (k_span == q_span) if flip == 0 else jnp.logical_and(seen, k_span < q_span)
        else:
            seen = jnp.logical_and(seen, quad + later < QUAD)

        @pl.when(seen)
        def _():
            scores = jnp.dot(kv_ref[0:span_len, :], q_t[...], preferred_element_type=jnp.float32)
            live = lax.broadcasted_iota(jnp.int32, scores.shape, 0) < counts_ref[k_span]
            scores = jnp.where(live, scores * factor, NEG_BIG)
            best = stat[0:1, :]
            top = jnp.maximum(best, jnp.max(scores, axis=0, keepdims=True))
            weights = jnp.exp2(scores - top)
            fading = jnp.exp2(best - top)
            stat[8:9, :] = stat[8:9, :] * fading + jnp.sum(weights, axis=0, keepdims=True)
            stat[0:1, :] = top
            values = jnp.concatenate(
                [kv_ref[span_len + b * HD : span_len + (b + 1) * HD, :] for b in range(span_len // HD)], axis=1
            )
            acc[...] = acc[...] * fading + jnp.dot(
                values, weights.astype(jnp.bfloat16), preferred_element_type=jnp.float32
            )


def begin_kernel(ids_ref, visible_ref, counts_ref, q0, q1, q2, q3, kv_ref, q_t, stat, acc):
    for later, q_ref in enumerate((q0, q1, q2, q3)):
        q_t[later] = jnp.transpose(q_ref[...])
        stat[later, 0:8, :] = jnp.full((8, stat.shape[2]), NEG_BIG, jnp.float32)
        stat[later, 8:16, :] = jnp.zeros((8, stat.shape[2]), jnp.float32)
        acc[later] = jnp.zeros(acc.shape[1:], jnp.float32)
        scan_keys(
            later, (0,), ids_ref, visible_ref, counts_ref, q_t.at[later], (kv_ref,), stat.at[later], acc.at[later]
        )


def middle_kernel(ids_ref, visible_ref, counts_ref, q_t, stat_in, acc_in, kv_ref, stat, acc):
    for later in range(QUAD):
        scan_keys(
            later, (2,), ids_ref, visible_ref, counts_ref, q_t.at[later], (kv_ref,), stat.at[later], acc.at[later]
        )


def finish_kernel(later, ids_ref, visible_ref, counts_ref, q_t, stat_in, acc_in, kv1, kv3, out_ref, stat, acc):
    span_len = out_ref.shape[0] - STAT_ROWS

    @pl.when(ids_ref[YH] + later < QUAD)
    def _():
        stat[...] = stat_in[later]
        acc[...] = acc_in[later]
        scan_keys(later, (1, 3), ids_ref, visible_ref, counts_ref, q_t.at[later], (kv1, kv3), stat, acc)
        best = stat[0:1, :]
        high = best.astype(jnp.bfloat16).astype(jnp.float32)
        low = (best - high).astype(jnp.bfloat16).astype(jnp.float32)
        scale = jnp.where(best > 0.5 * NEG_BIG, jnp.exp2((best - high) - low), 0.0)
        total = stat[8:9, :] * scale
        total_high = total.astype(jnp.bfloat16).astype(jnp.float32)
        stats = jnp.concatenate([high, low, total_high, total - total_high], axis=0)
        result = (acc[...] * scale).astype(jnp.bfloat16)
        for b in range(span_len // HD):
            out_ref[b * HD : (b + 1) * HD, :] = result[:, b * HD : (b + 1) * HD]
        stats = jnp.concatenate([stats[:, b * HD : (b + 1) * HD] for b in range(span_len // HD)], axis=0)
        out_ref[span_len:, :] = stats.astype(jnp.bfloat16)

    @pl.when(ids_ref[YH] + later >= QUAD)
    def _():
        out_ref[...] = jnp.zeros_like(out_ref)


def merge_kernel(ids_ref, counts_ref, part0, part1, part2, part3, out_ref):
    span_len = out_ref.shape[0]
    parts = (part0, part1, part2, part3)
    blocks = span_len // HD
    for block in range(blocks):
        bests, totals = [], []
        for earlier, part in enumerate(parts):
            stat = part[span_len:, :].astype(jnp.float32)[block * 4 : (block + 1) * 4, :]
            sent = ids_ref[YH] >= earlier
            bests.append(jnp.where(sent, stat[0:1] + stat[1:2], NEG_BIG))
            totals.append(jnp.where(sent, stat[2:3] + stat[3:4], 0.0))
        top = functools.reduce(jnp.maximum, bests)
        share = [jnp.exp2(b - top) for b in bests]
        total = sum(s * t for s, t in zip(share, totals))
        rows = slice(block * HD, (block + 1) * HD)
        result = sum(s * part[rows, :].astype(jnp.float32) for s, part in zip(share, parts))
        slot = lax.broadcasted_iota(jnp.int32, total.shape, 1) + block * HD
        result = jnp.where(slot < counts_ref[ids_ref[SPAN]], result / total, 0.0)
        out_ref[rows, :] = jnp.transpose(result).astype(jnp.bfloat16)


def on_device(tokens, queries, key_weight, value_weight, modulation, levels, visible, counts):
    span_id = lax.axis_index(SPAN_AXES)
    ids = jnp.stack(
        [
            span_id,
            lax.axis_index("yh"),
            lax.axis_index(("yl", "xl")),
            lax.axis_index(("yh", "yl")),
            lax.axis_index("xl"),
            lax.axis_index("xh"),
            lax.axis_index("z"),
            lax.axis_index("c"),
        ]
    ).astype(jnp.int32)
    span_len, feats = tokens.shape
    depth = key_weight.shape[0] // 2

    def rows_of(part):
        first = part * depth
        return jnp.concatenate(
            [lax.dynamic_slice_in_dim(w, first, depth, 0) for w in (key_weight, value_weight)], axis=1
        )

    core = lax.axis_index("c")
    w_own, w_other = rows_of(core), rows_of(1 - core)
    w_other, ids = lax.optimization_barrier((w_other, ids))
    w_chip = jnp.stack([w_own, shifted(w_other, "c", 2, 1)])
    w0 = stacked(w_chip, shifted(w_chip, "xl", 2, 1))

    a0 = jnp.transpose(tokens)
    x0 = stacked(a0, shifted(a0, "xh", 2, 1))

    q1, q2, q3 = (moved(queries, -later) for later in (1, 2, 3))
    w0, q1, q3 = lax.optimization_barrier((w0, q1, q3))

    x_up, x_down, w_up, w_down = [x0], [x0], [w0], [w0]
    y_axes = ("yh", "yl")
    for step in range(4):
        x_up.append(shifted(x_up[-1], "z", RING, 1))
        if step < 3:
            w_up.append(shifted(w_up[-1], y_axes, RING, 1))
            x_down.append(shifted(x_down[-1], "z", RING, -1))
        w_down.append(shifted(w_down[-1], y_axes, RING, -1))
    x_slots = [x0, x_down[1], x_down[2], x_down[3], x_up[4], x_up[3], x_up[2], x_up[1]]
    w_slots = [w0, w_down[1], w_down[2], w_down[3], w_down[4], w_up[3], w_up[2], w_up[1]]

    early = row_sums(x_slots[:4] + x_slots[5:])
    own_sums = row_sums([x_slots[4]], early)
    other_sums = shifted(own_sums, "c", 2, 1)
    table = pl.pallas_call(
        table_kernel,
        out_shape=jax.ShapeDtypeStruct((modulation.shape[1] // feats, feats), jnp.float32),
        in_specs=[SMEM, SMEM, VMEM],
        out_specs=VMEM,
        compiler_params=params(),
    )(levels, ids, modulation)
    normed = pl.pallas_call(
        norm_kernel,
        out_shape=jax.ShapeDtypeStruct((RING, 2, span_len, feats), jnp.bfloat16),
        in_specs=[SMEM] + [VMEM] * (3 + RING),
        out_specs=VMEM,
        compiler_params=params(),
    )(ids, own_sums, other_sums, table, *x_slots)
    near, far = (0, 1, 2, 3, 5, 6, 7), (4,)
    half = project(1, near, ids, normed, [w_slots[k] for k in near])
    half, q2 = lax.optimization_barrier((half, q2))
    theirs = shifted(project(1, far, ids, normed, [w_slots[4]], (half,)), "c", 2, 1)
    mine = project(0, tuple(range(RING)), ids, normed, w_slots)
    kv0 = pl.pallas_call(
        join_kernel,
        out_shape=jax.ShapeDtypeStruct((2 * span_len, HD), jnp.bfloat16),
        in_specs=[VMEM, VMEM],
        out_specs=VMEM,
        compiler_params=params(),
    )(mine, theirs)

    kv1 = shifted(kv0, "xl", 2, 1)
    kv2 = shifted(kv0, "yl", 2, 1)
    kv3 = lax.ppermute(kv0, ("yl", "xl"), [(i, 3 - i) for i in range(4)])
    scalars = (ids, visible, counts)
    q_type = jax.ShapeDtypeStruct((QUAD, HD, span_len), jnp.bfloat16)
    stat_type = jax.ShapeDtypeStruct((QUAD, 16, span_len), jnp.float32)
    acc_type = jax.ShapeDtypeStruct((QUAD, HD, span_len), jnp.float32)
    q_t, stat, acc = pl.pallas_call(
        begin_kernel,
        out_shape=(q_type, stat_type, acc_type),
        in_specs=[SMEM] * 3 + [VMEM] * 5,
        out_specs=(VMEM,) * 3,
        compiler_params=params(),
    )(*scalars, queries, q1, q2, q3, kv0)
    stat, acc = pl.pallas_call(
        middle_kernel,
        out_shape=(stat_type, acc_type),
        in_specs=[SMEM] * 3 + [VMEM] * 4,
        out_specs=(VMEM,) * 2,
        input_output_aliases={4: 0, 5: 1},
        compiler_params=params(),
    )(*scalars, q_t, stat, acc, kv2)
    parts = [None] * QUAD
    for later in (2, 3, 1, 0):
        part = pl.pallas_call(
            functools.partial(finish_kernel, later),
            out_shape=jax.ShapeDtypeStruct((span_len + STAT_ROWS, HD), jnp.bfloat16),
            in_specs=[SMEM] * 3 + [VMEM] * 5,
            out_specs=VMEM,
            scratch_shapes=[pltpu.VMEM((16, span_len), jnp.float32), pltpu.VMEM((HD, span_len), jnp.float32)],
            compiler_params=params(),
        )(*scalars, q_t, stat, acc, kv1, kv3)
        parts[later] = moved(part, later) if later else part
    return pl.pallas_call(
        merge_kernel,
        out_shape=jax.ShapeDtypeStruct((span_len, HD), jnp.bfloat16),
        in_specs=[SMEM, SMEM] + [VMEM] * QUAD,
        out_specs=VMEM,
        compiler_params=params(),
    )(ids, counts, *parts)


def solution(mesh):
    fine = Mesh(mesh.devices.reshape(SIZES), SPAN_AXES + FSDP_AXES)
    spread = P(SPAN_AXES, FSDP_AXES)
    return jax.shard_map(
        on_device,
        mesh=fine,
        in_specs=(spread, spread, spread, spread, P(), P(), P(), P()),
        out_specs=spread,
        check_vma=False,
    )
```
